32 devices in a mesh: gx: 8 (over y, x, core), gy: 4 (over z).
Axes of the slice: x: 2, y: 2, z: 4, core: 2. Of those that a mesh axis runs over, the one named last changes fastest.
Arguments:
- concentration: bfloat16 [128, 128, 512], P(None, 'gx', 'gy'), may hold values from 0.099609375 to 1
- adjoint_next: bfloat16 [128, 128, 512], P(None, 'gx', 'gy'), may hold values from 0 to 2
- sign_x: int32 [128, 512], P('gx', 'gy'), may hold values from 0 to 1
- sign_y: int32 [128, 512], P('gx', 'gy'), may hold values from 0 to 1
- courant_x: float32 [128, 512], P('gx', 'gy'), may hold values from 0.05 to 0.24
- courant_y: float32 [128, 512], P('gx', 'gy'), may hold values from 0.05 to 0.24
- active: int32 [128, 512], P('gx', 'gy'), may hold values from 0 to 1, as said below
- kernel_a: float32 [128], replicated, may hold values from 0.01 to 0.1
- kernel_b: float32 [128], replicated, may hold values from 0.01 to 0.1
Outputs:
- gradient: float32 [128, 128, 512], P(None, 'gx', 'gy')
The draws below stay inside these ranges and needn't reach their ends.
Inputs may be any that keep to these rules, and one draw needn't show every extreme that they name: Among the devices that share one gy index, 2 hold exactly 2048 active cells (all of their cells) and the others exactly 256; which devices hold more is drawn anew.
All inputs are finite; a program needn't handle non-finite values.
Results may differ from the reference program's by a relative error of at most 0.0003.
Values sent between devices are 32-bit elements; how exact they have to be, the bound alone decides.
A program may use at most 64 MiB of HBM per device.

```python
import math
import jax
import jax.numpy as jnp
from jax import lax

NB = 128
SUBSTEPS = 4
CX = 16
CY = 128
NX = 128
NY = 512
N_GX = 8
N_GY = 4


def draw_active(key, part):
    first_key, second_key = jax.random.split(key)
    busy_rank = jax.vmap(lambda subkey: jax.random.permutation(subkey, N_GX))(jax.random.split(first_key, N_GY))
    cell_total = CX * CY
    quota_cells = jnp.where(busy_rank < N_GX // 4, cell_total, cell_total // 8)
    shuffled = jax.vmap(lambda subkey: jax.random.permutation(subkey, cell_total))(jax.random.split(second_key, N_GY * N_GX))
    shuffled = shuffled.reshape(N_GY, N_GX, cell_total)
    chosen = (shuffled < quota_cells[:, :, None]).astype(jnp.int32)
    chosen = chosen.reshape(N_GY, N_GX, CX, CY).transpose(1, 2, 0, 3).reshape(N_GX * CX, N_GY * CY)
    return chosen


def touch_ends(drawn, stream_key, low, top_value):
    shape = drawn.shape
    place = [jax.random.randint(jax.random.fold_in(stream_key, axis), (), 0, shape[axis]) for axis in range(len(shape))]
    drawn = drawn.at[tuple(place)].set(low)
    longest = shape.index(max(shape))
    place[longest] = (place[longest] + 1) % shape[longest]
    return drawn.at[tuple(place)].set(top_value)


def level_of(own_key, shape, shards, smallest, high):
    def one(axis_at, parts):
        draws = jax.random.uniform(jax.random.fold_in(jax.random.fold_in(own_key, 6), axis_at), (parts,), jnp.float32, smallest / len(shards), high / len(shards))
        return jnp.repeat(jnp.exp(draws), shape[axis_at] // parts).reshape((-1,) + (1,) * (len(shape) - axis_at - 1))

    level = one(*shards[0])
    for cut in shards[1:]:
        level = level * one(*cut)
    return level


def setup_inputs(seed: int = 0) -> dict:
    key_of = jax.random.split(jax.random.key(seed), 10)
    return {
        "concentration": jnp.clip(jnp.exp(math.log(1.0) - 2.306499 * jax.random.uniform(key_of[0], (NB, NX, NY), jnp.float32) ** level_of(key_of[0], (NB, NX, NY), ((1, 8), (2, 4)), -0.2, 0.2)), 0.099609375, 1.0).astype(jnp.bfloat16),
        "adjoint_next": jnp.clip(2.0 * jax.random.uniform(key_of[1], (NB, NX, NY), jnp.float32) ** level_of(key_of[1], (NB, NX, NY), ((1, 8), (2, 4)), -0.2, 0.2), 0.0, 2.0).astype(jnp.bfloat16),
        "sign_x": touch_ends(jax.random.randint(key_of[2], (NX, NY), 0, 2), jax.random.fold_in(key_of[2], 1), 0, 1).astype(jnp.int32),
        "sign_y": touch_ends(jax.random.randint(key_of[3], (NX, NY), 0, 2), jax.random.fold_in(key_of[3], 1), 0, 1).astype(jnp.int32),
        "courant_x": jnp.clip(0.05 + 0.19 * jax.random.uniform(key_of[4], (NX, NY), jnp.float32) ** level_of(key_of[4], (NX, NY), ((0, 8), (1, 4)), -0.2, 0.2), 0.05, 0.24),
        "courant_y": jnp.clip(0.05 + 0.19 * jax.random.uniform(key_of[5], (NX, NY), jnp.float32) ** level_of(key_of[5], (NX, NY), ((0, 8), (1, 4)), -0.2, 0.2), 0.05, 0.24),
        "active": draw_active(jax.random.fold_in(key_of[9], 71), 0),
        "kernel_a": jnp.clip(jnp.exp(jax.random.uniform(key_of[7], (NB,), jnp.float32, math.log(0.01), math.log(0.1))), 0.01, 0.1),
        "kernel_b": jnp.clip(jnp.exp(jax.random.uniform(key_of[8], (NB,), jnp.float32, math.log(0.01), math.log(0.1))), 0.01, 0.1),
    }


def face_weights(sign_x, sign_y, courant_x, courant_y):
    plus_x = sign_x.astype(jnp.float32)
    plus_y = sign_y.astype(jnp.float32)
    column = jnp.arange(NY, dtype=jnp.int32)[None, :]
    inside = (column > 0).astype(jnp.float32)
    return (courant_x * plus_x, courant_x * (1.0 - plus_x), courant_y * plus_y * inside, courant_y * (1.0 - plus_y) * inside)


def after_x(field):
    return jnp.roll(field, -1, axis=-2)


def before_x(field):
    return jnp.roll(field, 1, axis=-2)


def after_y(field):
    return jnp.concatenate([field[..., 1:], jnp.zeros_like(field[..., :1])], axis=-1)


def before_y(field):
    return jnp.concatenate([jnp.zeros_like(field[..., :1]), field[..., :-1]], axis=-1)


def transport_forward(field, weights):
    upward_x, backward_x, upward_y, backward_y = weights
    return (field + upward_x * before_x(field) - (backward_x + after_x(upward_x)) * field + after_x(backward_x) * after_x(field)
            + upward_y * before_y(field) - (backward_y + after_y(upward_y)) * field + after_y(backward_y) * after_y(field))


def transport_adjoint(field, weights):
    upward_x, backward_x, upward_y, backward_y = weights
    return (field * (1.0 - backward_x - after_x(upward_x) - backward_y - after_y(upward_y))
            + after_x(upward_x) * after_x(field) + backward_x * before_x(field)
            + after_y(upward_y) * after_y(field) + backward_y * before_y(field))


def spectrum(values):
    return jnp.fft.rfft(values, n=2 * NB, axis=0)


def gain_terms(spectra_a, spectra_b):
    full = jnp.fft.irfft(spectra_a * spectra_b, n=2 * NB, axis=0)
    return jnp.concatenate([jnp.zeros_like(full[:1]), full[:NB - 1]], axis=0)


def lag_terms(spectra_l, spectra_v):
    full = jnp.fft.irfft(spectra_l * jnp.conj(spectra_v), n=2 * NB, axis=0)
    return full[1:NB + 1]


def coagulation(column_state, column_adjoint, mask_row, kernel_a, kernel_b):
    weight_a = kernel_a[:, None]
    weight_b = kernel_b[:, None]
    current = column_state
    saved = []
    for substep in range(SUBSTEPS):
        scaled_a = weight_a * current
        scaled_b = weight_b * current
        spectra_a = spectrum(scaled_a)
        spectra_b = spectrum(scaled_b)
        total_a = jnp.sum(scaled_a, axis=0, keepdims=True)
        total_b = jnp.sum(scaled_b, axis=0, keepdims=True)
        saved.append((current, spectra_a, spectra_b, total_a, total_b))
        if substep < SUBSTEPS - 1:
            gained = gain_terms(spectra_a, spectra_b)
            current = current + mask_row * (gained - current * (weight_a * total_b + weight_b * total_a))
    adjoint = column_adjoint
    for substep in reversed(range(SUBSTEPS)):
        current, spectra_a, spectra_b, total_a, total_b = saved[substep]
        spectra_l = spectrum(adjoint)
        grad_a = lag_terms(spectra_l, spectra_b)
        grad_b = lag_terms(spectra_l, spectra_a)
        moment_a = jnp.sum(adjoint * current * weight_a, axis=0, keepdims=True)
        moment_b = jnp.sum(adjoint * current * weight_b, axis=0, keepdims=True)
        change = (weight_a * grad_a + weight_b * grad_b - adjoint * (weight_a * total_b + weight_b * total_a)
                  - weight_b * moment_a - weight_a * moment_b)
        adjoint = adjoint + mask_row * change
    return adjoint


def reference(concentration, adjoint_next, sign_x, sign_y, courant_x, courant_y, active, kernel_a, kernel_b):
    weights = face_weights(sign_x, sign_y, courant_x, courant_y)
    moved = transport_forward(concentration.astype(jnp.float32), weights)
    adjoint_end = adjoint_next.astype(jnp.float32)
    mask_all = active.astype(jnp.float32)

    def one_row(packed):
        row_state, row_adjoint, row_mask = packed
        return coagulation(row_state, row_adjoint, row_mask[None, :], kernel_a, kernel_b)

    rows_out = lax.map(one_row, (jnp.moveaxis(moved, 1, 0), jnp.moveaxis(adjoint_end, 1, 0), mask_all))
    adjoint_mid = jnp.moveaxis(rows_out, 0, 1)
    return transport_adjoint(adjoint_mid, weights)
```

```python
import functools

import jax
import jax.numpy as jnp
import numpy as np
from jax import lax
from jax.experimental import pallas as pl
from jax.experimental.pallas import tpu as pltpu
from jax.sharding import PartitionSpec as P

SUBSTEPS = 4
PART = 16
BLOCK = 8
F32 = jnp.float32
BF16 = jnp.bfloat16


def dft_tables(bins):
    order = np.arange(bins)
    order = np.concatenate([order[:PART // 2], order[-(PART // 2):], order[PART // 2:-(PART // 2)]])
    freq = 2 * order + 1
    index = np.arange(bins)

    def chunked(real, imag):
        pieces = [t[c:c + PART] for c in range(0, bins, PART) for t in (real, imag)]
        return np.concatenate(pieces, axis=0)

    angle = np.pi * (freq[:, None] * index[None, :] % (4 * bins)) / (2 * bins)
    forward = chunked(np.cos(angle), -np.sin(angle))

    def inverse(outputs):
        phase = np.pi * (freq[:, None] * outputs[None, :] % (4 * bins)) / (2 * bins)
        return chunked(np.cos(phase), -np.sin(phase)).T / bins

    gain = inverse(index - 1) * (index > 0)[:, None]
    lag = inverse(index + 1) - inverse(0 * index)
    return tuple(np.asarray(t, np.float32) for t in (forward, gain, lag))


def split(values):
    high = values.astype(BF16)
    low = (values - high.astype(F32)).astype(BF16)
    return high, low


def dot(table, values):
    return jnp.dot(table, values, preferred_element_type=F32)


def rows(*values):
    return jnp.concatenate(values, axis=0)


def product(ar, ai, br, bi):
    return rows(ar * br - ai * bi, ar * bi + ai * br)


def product_conj(lr, li, vr, vi):
    return rows(lr * vr + li * vi, li * vr - lr * vi)


def quarters(chunk):
    return tuple(chunk[q * PART:(q + 1) * PART] for q in range(chunk.shape[0] // PART))


def high_low(chunks):
    high, low = split(chunks[0])
    return [high, *(c.astype(BF16) for c in chunks[1:])], low


def kernel(
    n_gx, n_gy, width_x,
    *refs,
):
    inputs, refs = refs[:12], refs[12:]
    out, refs = refs[0], refs[1:]
    fetched, refs = refs[:12], refs[12:]
    conc, adj, sx, sy, cx, cy, active, ka_ref, kb_ref, fwd_ref, gain_ref, lag_ref = fetched
    (wide, wide_adj, state, lam, y_send, y_recv, z_send, z_recv, moved, faces, t_fwd, t_gain, t_lam, t_lag, weights,
     send_sem, recv_sem, in_sem) = refs
    fetches = [pltpu.make_async_copy(i, f, in_sem.at[k]) for k, (i, f) in enumerate(zip(inputs, fetched))]
    for k in (0, 2, 3, 4, 5, 1, 7, 8, 9, 10, 11, 6):
        fetches[k].start()
    bins = ka_ref.shape[1]
    width_y = sx.shape[1]
    gx = lax.axis_index("gx")
    gy = lax.axis_index("gy")
    nxt_x, prv_x = lax.rem(gx + 1, n_gx), lax.rem(gx + n_gx - 1, n_gx)
    nxt_y, prv_y = jnp.minimum(gy + 1, n_gy - 1), jnp.maximum(gy - 1, 0)
    has_prv, has_nxt = gy > 0, gy < n_gy - 1
    mesh_id = pl.DeviceIdType.MESH

    barrier = pltpu.get_barrier_semaphore()
    pl.semaphore_signal(barrier, inc=1, device_id=(prv_x, gy), device_id_type=mesh_id)
    pl.semaphore_signal(barrier, inc=1, device_id=(nxt_x, gy), device_id_type=mesh_id)

    @pl.when(has_prv)
    def _():
        pl.semaphore_signal(barrier, inc=1, device_id=(gx, prv_y), device_id_type=mesh_id)

    @pl.when(has_nxt)
    def _():
        pl.semaphore_signal(barrier, inc=1, device_id=(gx, nxt_y), device_id_type=mesh_id)

    lane = lax.broadcasted_iota(jnp.int32, (bins, width_y), 1)
    lane_x = lax.broadcasted_iota(jnp.int32, (width_x, width_y), 1)

    for k in (2, 3, 4, 5):
        fetches[k].wait()
    plus_x = sx[...].astype(F32)
    plus_y = sy[...].astype(F32)
    inside = (lane_x + gy * width_y > 0).astype(F32)
    ux = cx[...] * plus_x
    bx = cx[...] * (1.0 - plus_x)
    uy = cy[...] * plus_y * inside
    by = cy[...] * (1.0 - plus_y) * inside

    fetches[0].wait()
    wide[...] = conc[...].astype(F32)
    for x in (0, width_x - 1):
        state[x + 1, :bins, :] = wide[pl.ds(x, bins, stride=width_x), :]
    state[1, bins:bins + 1, :] = ux[0:1]
    state[1, bins + 1:bins + 2, :] = bx[0:1]
    state[1, bins + 2:, :] = jnp.zeros((6, width_y), F32)
    state[width_x, bins:, :] = jnp.zeros((8, width_y), F32)

    def x_copies(field, base):
        return (
            pltpu.make_async_remote_copy(
                src_ref=field.at[1], dst_ref=field.at[width_x + 1],
                send_sem=send_sem.at[base], recv_sem=recv_sem.at[base],
                device_id=(prv_x, gy), device_id_type=mesh_id),
            pltpu.make_async_remote_copy(
                src_ref=field.at[width_x], dst_ref=field.at[0],
                send_sem=send_sem.at[base + 1], recv_sem=recv_sem.at[base + 1],
                device_id=(nxt_x, gy), device_id_type=mesh_id),
        )

    pl.semaphore_wait(barrier, 2 + has_prv.astype(jnp.int32) + has_nxt.astype(jnp.int32))
    first_x = x_copies(state, 0)
    for copy in first_x:
        copy.start()
    for x in range(1, width_x - 1):
        state[x + 1, :bins, :] = wide[pl.ds(x, bins, stride=width_x), :]

    def edges(field, places):
        to_prv = jnp.zeros((bins, width_y), F32)
        to_nxt = jnp.zeros((bins, width_y), F32)
        for x in places:
            slab = field[x + 1, :bins, :]
            to_prv = jnp.where(lane == x, pltpu.roll(slab, x, 1), to_prv)
            to_nxt = jnp.where(lane == x, pltpu.roll(slab, x + 1, 1), to_nxt)
        return to_prv, to_nxt

    y_send[0, :bins, :], y_send[1, :bins, :] = edges(state, range(width_x))
    y_send[0, bins:bins + width_x, :] = uy
    y_send[0, bins + width_x:, :] = by
    y_send[1, bins:, :] = jnp.zeros((2 * width_x, width_y), F32)

    def y_copies(source, target, base):
        return (
            pltpu.make_async_remote_copy(
                src_ref=source.at[0], dst_ref=target.at[1],
                send_sem=send_sem.at[base], recv_sem=recv_sem.at[base],
                device_id=(gx, prv_y), device_id_type=mesh_id),
            pltpu.make_async_remote_copy(
                src_ref=source.at[1], dst_ref=target.at[0],
                send_sem=send_sem.at[base + 1], recv_sem=recv_sem.at[base + 1],
                device_id=(gx, nxt_y), device_id_type=mesh_id),
        )

    def start_y(copies, target):
        to_prv, to_nxt = copies

        @pl.when(has_prv)
        def _():
            to_prv.start()

        @pl.when(has_nxt)
        def _():
            to_nxt.start()

        @pl.when(jnp.logical_not(has_prv))
        def _():
            target[0] = jnp.zeros(target.shape[1:], F32)

        @pl.when(jnp.logical_not(has_nxt))
        def _():
            target[1] = jnp.zeros(target.shape[1:], F32)

    def wait_y(copies):
        to_prv, to_nxt = copies

        @pl.when(has_prv)
        def _():
            to_prv.wait_send()
            to_nxt.wait_recv()

        @pl.when(has_nxt)
        def _():
            to_nxt.wait_send()
            to_prv.wait_recv()

    first_y = y_copies(y_send, y_recv, 2)
    start_y(first_y, y_recv)

    for k in (7, 8, 9, 10, 11):
        fetches[k].wait()
    ka_row, kb_row = ka_ref[...], kb_ref[...]
    weights[0] = jnp.broadcast_to(ka_row, (bins, bins)).T
    weights[1] = jnp.broadcast_to(kb_row, (bins, bins)).T
    ka_col, kb_col = weights[0], weights[1]
    first, corrected = 2 * PART, 4 * PART
    forward = fwd_ref[...]
    ah, al = split(forward * ka_row)
    bh, bl = split(forward * kb_row)
    lh, ll = split(forward)
    blank = jnp.zeros((PART, bins), BF16)
    for c in range(bins // PART):
        for q, high in enumerate((ah, bh)):
            there = slice(c * corrected + q * first, c * corrected + (q + 1) * first)
            t_fwd[there, :bins] = high[c * first:(c + 1) * first]
            t_fwd[there, bins:] = high[c * first:(c + 1) * first]
    sums, rest = 4 * bins, 4 * bins + PART
    high, low = split(rows(ka_row, kb_row, jnp.zeros((PART - 2, bins), F32)))
    t_fwd[sums:rest, :bins] = high
    t_fwd[sums:rest, bins:] = high
    t_fwd[rest:, :bins] = rows(al[:first], bl[:first], low)
    t_fwd[rest:, bins:] = rows(*[blank] * 5)
    t_lam[:2 * bins, :bins] = lh
    t_lam[:2 * bins, bins:] = lh
    t_lam[2 * bins:, :bins] = ll[:first]
    t_lam[2 * bins:, bins:] = rows(blank, blank)
    high, low = split(gain_ref[...])
    t_gain[:, :2 * bins] = high
    t_gain[:, 2 * bins:2 * bins + first] = high[:, :first]
    t_gain[:, 2 * bins + first:] = low[:, :first]
    lag = lag_ref[...]
    ka_col2 = jnp.concatenate([ka_col, ka_col], axis=1)
    kb_col2 = jnp.concatenate([kb_col, kb_col], axis=1)
    ah, al = split(ka_col2 * lag)
    bh, bl = split(kb_col2 * lag)
    t_lag[:, :2 * bins] = ah
    t_lag[:, 2 * bins:4 * bins] = bh
    t_lag[:, 4 * bins:] = jnp.concatenate([ah[:, :first], bh[:, :first], al[:, :first], bl[:, :first]], axis=1)

    fetches[1].wait()
    fetches[6].wait()
    wide_adj[...] = adj[...].astype(F32)
    for x in range(width_x):
        lam[x + 1, :bins, :] = wide_adj[pl.ds(x, bins, stride=width_x), :]

    wait_y(first_y)
    for copy in first_x:
        copy.wait()

    ux_next = jnp.concatenate([ux[1:], state[width_x + 1, bins:bins + 1, :]], axis=0)
    bx_next = jnp.concatenate([bx[1:], state[width_x + 1, bins + 1:bins + 2, :]], axis=0)
    last_lane = lane_x == width_y - 1
    uy_next = jnp.where(
        last_lane, pltpu.roll(y_recv[1, bins:bins + width_x, :], width_y - 1, 1), pltpu.roll(uy, width_y - 1, 1))
    by_next = jnp.where(
        last_lane, pltpu.roll(y_recv[1, bins + width_x:, :], width_y - 1, 1), pltpu.roll(by, width_y - 1, 1))
    centre = 1.0 - bx - ux_next - by - uy_next
    for index, values in enumerate((centre, ux, bx, ux_next, bx_next, uy, by, uy_next, by_next)):
        faces[index] = values

    def stencil(field, halo, x, low_x, high_x, low_y, high_y):
        slab = field[x + 1, :bins, :]
        before = jnp.where(lane == 0, pltpu.roll(halo[0, :bins, :], (width_y - x) % width_y, 1), pltpu.roll(slab, 1, 1))
        after = jnp.where(
            lane == width_y - 1, pltpu.roll(halo[1, :bins, :], width_y - 1 - x, 1), pltpu.roll(slab, width_y - 1, 1))
        row = lambda k: faces[k, x:x + 1, :]
        return (
            slab * row(0)
            + row(low_x) * field[x, :bins, :]
            + row(high_x) * field[x + 2, :bins, :]
            + row(low_y) * before
            + row(high_y) * after
        )

    for x in range(width_x):
        moved[x] = stencil(state, y_recv, x, 1, 4, 5, 8)

    lam[1, bins:, :] = jnp.zeros((8, width_y), F32)
    lam[width_x, bins:, :] = jnp.zeros((8, width_y), F32)
    half, quarter = width_x // 2, width_x // 4
    second_x = x_copies(lam, 4)

    def second_y(group):
        return y_copies(z_send.at[group], z_recv.at[group], 6 + 2 * group)

    def coagulate(block):
        beside = lambda values: jnp.concatenate(list(values), axis=1)
        current = beside(moved[x] for x in block)
        start = beside(lam[x + 1, :bins, :] for x in block)
        ka = beside(weights[0] for _ in block)
        kb = beside(weights[1] for _ in block)
        saved = []
        for step in range(SUBSTEPS):
            high, low = split(current)
            result = dot(t_fwd[...], rows(high, low))
            spectra = [result[c:c + corrected] for c in range(0, sums, corrected)]
            spectra[0] = spectra[0] + result[rest:rest + corrected]
            spectra = [quarters(chunk) for chunk in spectra]
            total_a, total_b = (
                result[sums + k:sums + k + 1] + result[rest + corrected + k:rest + corrected + k + 1] for k in (0, 1))
            loss = ka * total_b + kb * total_a
            saved.append((spectra, loss))
            if step < SUBSTEPS - 1:
                high, low = high_low([product(*chunk) for chunk in spectra])
                current = current + dot(t_gain[...], rows(*high, low, high[0])) - current * loss
        adjoint = start
        for step in reversed(range(SUBSTEPS)):
            spectra, loss = saved[step]
            high, low = split(adjoint)
            result = dot(t_lam[...], rows(high, low))
            spectra_l = [result[c:c + first] for c in range(0, 2 * bins, first)]
            spectra_l[0] = spectra_l[0] + result[2 * bins:]
            spectra_l = [quarters(chunk) for chunk in spectra_l]
            high_b, low_b = high_low([product_conj(*l, *v[2:]) for l, v in zip(spectra_l, spectra)])
            high_a, low_a = high_low([product_conj(*l, *v[:2]) for l, v in zip(spectra_l, spectra)])
            terms = rows(*high_b, *high_a, low_b, low_a, high_b[0], high_a[0])
            adjoint = adjoint + dot(t_lag[...], terms) - adjoint * loss
        on = beside(active[pl.ds(x, 1), :] for x in block) == 1
        result = jnp.where(on, adjoint, start)
        for index, x in enumerate(block):
            lam[x + 1, :bins, :] = result[:, index * width_y:(index + 1) * width_y]

    @pl.loop(0, 2)
    def _(group):
        places = [p + quarter * group for p in range(quarter)]
        places += [p + half - quarter * group for p in range(quarter, half)]
        for pick in range(0, half, BLOCK):
            coagulate(places[pick:pick + BLOCK])

        @pl.when(group == 0)
        def _():
            for copy in second_x:
                copy.start()

        z_send[group, 0], z_send[group, 1] = edges(lam, places)
        start_y(second_y(group), z_recv.at[group])

    outer = [*range(quarter), *range(half + quarter, width_x)]
    for copy in second_x:
        copy.wait()
    for group, places in enumerate((outer, range(quarter, half + quarter))):
        wait_y(second_y(group))
        for x in places:
            out[pl.ds(x, bins, stride=width_x), :] = stencil(lam, z_recv.at[group], x, 2, 3, 6, 7)


def body(n_gx, n_gy, concentration, adjoint_next, sign_x, sign_y, courant_x, courant_y, active, kernel_a, kernel_b):
    bins, width_x, width_y = concentration.shape
    cells = bins * width_x
    tables = dft_tables(bins)
    operands = (
        concentration.reshape(cells, width_y),
        adjoint_next.reshape(cells, width_y),
        sign_x, sign_y, courant_x, courant_y, active,
        kernel_a.reshape(1, bins), kernel_b.reshape(1, bins),
        *(jnp.asarray(t) for t in tables),
    )
    result = pl.pallas_call(
        functools.partial(kernel, n_gx, n_gy, width_x),
        out_shape=pltpu.VMEM((cells, width_y), F32),
        in_specs=[pl.BlockSpec(memory_space=pltpu.HBM)] * 12,
        out_specs=pl.BlockSpec(memory_space=pltpu.VMEM),
        scratch_shapes=[
            *(pltpu.VMEM(a.shape, a.dtype) for a in operands),
            pltpu.VMEM((cells, width_y), F32),
            pltpu.VMEM((cells, width_y), F32),
            pltpu.VMEM((width_x + 2, bins + 8, width_y), F32),
            pltpu.VMEM((width_x + 2, bins + 8, width_y), F32),
            pltpu.VMEM((2, bins + 2 * width_x, width_y), F32),
            pltpu.VMEM((2, bins + 2 * width_x, width_y), F32),
            pltpu.VMEM((2, 2, bins, width_y), F32),
            pltpu.VMEM((2, 2, bins, width_y), F32),
            pltpu.VMEM((width_x, bins, width_y), F32),
            pltpu.VMEM((9, width_x, width_y), F32),
            pltpu.VMEM((4 * bins + 6 * PART, 2 * bins), BF16),
            pltpu.VMEM((bins, 2 * bins + 4 * PART), BF16),
            pltpu.VMEM((2 * bins + 2 * PART, 2 * bins), BF16),
            pltpu.VMEM((bins, 4 * bins + 8 * PART), BF16),
            pltpu.VMEM((2, bins, bins), F32),
            pltpu.SemaphoreType.DMA((10,)),
            pltpu.SemaphoreType.DMA((10,)),
            pltpu.SemaphoreType.DMA((12,)),
        ],
        compiler_params=pltpu.CompilerParams(
            collective_id=0, has_side_effects=True, vmem_limit_bytes=60 * 1024 * 1024
        ),
    )(*operands)
    return result.reshape(bins, width_x, width_y)


def solution(mesh):
    return jax.shard_map(
        functools.partial(body, mesh.shape["gx"], mesh.shape["gy"]),
        mesh=mesh,
        in_specs=(
            P(None, "gx", "gy"),
            P(None, "gx", "gy"),
            P("gx", "gy"),
            P("gx", "gy"),
            P("gx", "gy"),
            P("gx", "gy"),
            P("gx", "gy"),
            P(),
            P(),
        ),
        out_specs=P(None, "gx", "gy"),
        check_vma=False,
    )
```

```python
import functools

import jax
import jax.numpy as jnp
import numpy as np
from jax import lax
from jax.experimental import pallas as pl
from jax.experimental.pallas import tpu as pltpu
from jax.sharding import PartitionSpec as P

SUBSTEPS = 4
PART = 16
EARLY = 8
MIDDLE = 1
F32 = jnp.float32
BF16 = jnp.bfloat16


def dft_tables(bins):
    order = np.arange(bins)
    order = np.concatenate([order[:PART // 2], order[-(PART // 2):], order[PART // 2:-(PART // 2)]])
    freq = 2 * order + 1
    index = np.arange(bins)

    def chunked(real, imag):
        pieces = [t[c:c + PART] for c in range(0, bins, PART) for t in (real, imag)]
        return np.concatenate(pieces, axis=0)

    angle = np.pi * (freq[:, None] * index[None, :] % (4 * bins)) / (2 * bins)
    forward = chunked(np.cos(angle), -np.sin(angle))

    def inverse(outputs):
        phase = np.pi * (freq[:, None] * outputs[None, :] % (4 * bins)) / (2 * bins)
        return chunked(np.cos(phase), -np.sin(phase)).T / bins

    gain = inverse(index - 1) * (index > 0)[:, None]
    lag = inverse(index + 1) - inverse(0 * index)
    return tuple(np.asarray(t, np.float32) for t in (forward, gain, lag))


def split(values):
    high = values.astype(BF16)
    low = (values - high.astype(F32)).astype(BF16)
    return high, low


def dot(table, values):
    return jnp.dot(table, values, preferred_element_type=F32)


def rows(*values):
    return jnp.concatenate(values, axis=0)


def product(ar, ai, br, bi):
    return rows(ar * br - ai * bi, ar * bi + ai * br)


def product_conj(lr, li, vr, vi):
    return rows(lr * vr + li * vi, li * vr - lr * vi)


def quarters(chunk):
    return tuple(chunk[q * PART:(q + 1) * PART] for q in range(chunk.shape[0] // PART))


def high_low(chunks):
    high, low = split(chunks[0])
    return [high, *(c.astype(BF16) for c in chunks[1:])], low


def kernel(
    n_gx, n_gy, width_x,
    *refs,
):
    inputs, refs = refs[:12], refs[12:]
    out, refs = refs[0], refs[1:]
    fetched, refs = refs[:12], refs[12:]
    conc, adj, sx, sy, cx, cy, active, ka_ref, kb_ref, fwd_ref, gain_ref, lag_ref = fetched
    (wide, wide_adj, state, lam, y_send, y_recv, z_send, z_recv, faces, t_fwd, t_gain, t_lam, t_lag, weights,
     send_sem, recv_sem, in_sem) = refs
    fetches = [pltpu.make_async_copy(i, f, in_sem.at[k]) for k, (i, f) in enumerate(zip(inputs, fetched))]
    for k in (0, 2, 3, 4, 5, 1, 7, 8, 9, 10, 11, 6):
        fetches[k].start()
    bins = ka_ref.shape[1]
    width_y = sx.shape[1]
    gx = lax.axis_index("gx")
    gy = lax.axis_index("gy")
    nxt_x, prv_x = lax.rem(gx + 1, n_gx), lax.rem(gx + n_gx - 1, n_gx)
    nxt_y, prv_y = jnp.minimum(gy + 1, n_gy - 1), jnp.maximum(gy - 1, 0)
    has_prv, has_nxt = gy > 0, gy < n_gy - 1
    mesh_id = pl.DeviceIdType.MESH

    barrier = pltpu.get_barrier_semaphore()
    pl.semaphore_signal(barrier, inc=1, device_id=(prv_x, gy), device_id_type=mesh_id)
    pl.semaphore_signal(barrier, inc=1, device_id=(nxt_x, gy), device_id_type=mesh_id)

    @pl.when(has_prv)
    def _():
        pl.semaphore_signal(barrier, inc=1, device_id=(gx, prv_y), device_id_type=mesh_id)

    @pl.when(has_nxt)
    def _():
        pl.semaphore_signal(barrier, inc=1, device_id=(gx, nxt_y), device_id_type=mesh_id)

    span = width_y // width_x
    lane = lax.broadcasted_iota(jnp.int32, (bins, width_y), 1)
    owner, place = lane // span, lane % span
    lane_x = lax.broadcasted_iota(jnp.int32, (width_x, width_y), 1)
    owner_x = lane_x // span

    def pack(slab_of, owners):
        packed = slab_of(0)
        packed = pltpu.roll(packed, span // 2, 1)
        for x in range(1, width_x):
            packed = jnp.where(owners == x, pltpu.roll(slab_of(x), x * span + span // 2, 1), packed)
        return packed

    def unpack(packed, x):
        return pltpu.roll(packed, width_y - x * span - span // 2, 1)

    for k in (2, 3, 4, 5):
        fetches[k].wait()
    plus_x = sx[...].astype(F32)
    plus_y = sy[...].astype(F32)
    inside = (lane_x + gy * width_y > 0).astype(F32)
    ux = cx[...] * plus_x
    bx = cx[...] * (1.0 - plus_x)
    uy = cy[...] * plus_y * inside
    by = cy[...] * (1.0 - plus_y) * inside

    def put_faces(ux_after, bx_after, uy_last, by_last):
        ux_next = rows(ux[1:], ux_after)
        bx_next = rows(bx[1:], bx_after)
        last_lane = lane_x == width_y - 1
        uy_next = jnp.where(last_lane, uy_last, pltpu.roll(uy, width_y - 1, 1))
        by_next = jnp.where(last_lane, by_last, pltpu.roll(by, width_y - 1, 1))
        centre = 1.0 - bx - ux_next - by - uy_next
        for index, values in enumerate((uy, by, ux, bx, ux_next, bx_next, uy_next, by_next, centre)):
            for x in range(width_x):
                faces[x, index:index + 1, :] = values[x:x + 1]

    for x in range(width_x):
        faces[x, 8:, :] = jnp.zeros((8, width_y), F32)
    put_faces(ux[:1], bx[:1], uy, by)

    fetches[0].wait()
    wide[...] = conc[...].astype(F32)
    for x in (0, width_x - 1):
        state[x + 1, :bins, :] = wide[pl.ds(x, bins, stride=width_x), :]
    state[1, bins:bins + 1, :] = ux[0:1]
    state[1, bins + 1:bins + 2, :] = bx[0:1]
    state[1, bins + 2:, :] = jnp.zeros((6, width_y), F32)
    state[width_x, bins:, :] = jnp.zeros((8, width_y), F32)

    def x_copies(field, base):
        return (
            pltpu.make_async_remote_copy(
                src_ref=field.at[1], dst_ref=field.at[width_x + 1],
                send_sem=send_sem.at[base], recv_sem=recv_sem.at[base],
                device_id=(prv_x, gy), device_id_type=mesh_id),
            pltpu.make_async_remote_copy(
                src_ref=field.at[width_x], dst_ref=field.at[0],
                send_sem=send_sem.at[base + 1], recv_sem=recv_sem.at[base + 1],
                device_id=(nxt_x, gy), device_id_type=mesh_id),
        )

    pl.semaphore_wait(barrier, 2 + has_prv.astype(jnp.int32) + has_nxt.astype(jnp.int32))
    first_x = x_copies(state, 0)
    for copy in first_x:
        copy.start()
    for x in range(1, width_x - 1):
        state[x + 1, :bins, :] = wide[pl.ds(x, bins, stride=width_x), :]

    y_send[:bins, :] = pack(lambda x: state[x + 1, :bins, :], owner)
    y_send[bins:, :] = pack(lambda x: faces[x, :8, :], owner[:8])

    def y_copies(source, target, base):
        return (
            pltpu.make_async_remote_copy(
                src_ref=source, dst_ref=target.at[1],
                send_sem=send_sem.at[base], recv_sem=recv_sem.at[base],
                device_id=(gx, prv_y), device_id_type=mesh_id),
            pltpu.make_async_remote_copy(
                src_ref=source, dst_ref=target.at[0],
                send_sem=send_sem.at[base + 1], recv_sem=recv_sem.at[base + 1],
                device_id=(gx, nxt_y), device_id_type=mesh_id),
        )

    def start_y(copies, target):
        to_prv, to_nxt = copies

        @pl.when(has_prv)
        def _():
            to_prv.start()

        @pl.when(has_nxt)
        def _():
            to_nxt.start()

        @pl.when(jnp.logical_not(has_prv))
        def _():
            target[0] = jnp.zeros(target.shape[1:], F32)

        @pl.when(jnp.logical_not(has_nxt))
        def _():
            target[1] = jnp.zeros(target.shape[1:], F32)

    def wait_y(copies):
        to_prv, to_nxt = copies

        @pl.when(has_prv)
        def _():
            to_prv.wait_send()
            to_nxt.wait_recv()

        @pl.when(has_nxt)
        def _():
            to_nxt.wait_send()
            to_prv.wait_recv()

    first_y = y_copies(y_send, y_recv, 2)
    start_y(first_y, y_recv)

    for k in (7, 8, 9, 10, 11):
        fetches[k].wait()
    ka_row, kb_row = ka_ref[...], kb_ref[...]
    weights[0] = jnp.broadcast_to(ka_row, (bins, bins)).T
    weights[1] = jnp.broadcast_to(kb_row, (bins, bins)).T
    ka_col, kb_col = weights[0], weights[1]
    first, corrected = 2 * PART, 4 * PART
    forward = fwd_ref[...]
    ah, al = split(forward * ka_row)
    bh, bl = split(forward * kb_row)
    lh, ll = split(forward)
    blank = jnp.zeros((PART, bins), BF16)
    for c in range(bins // PART):
        for q, high in enumerate((ah, bh)):
            there = slice(c * corrected + q * first, c * corrected + (q + 1) * first)
            t_fwd[there, :bins] = high[c * first:(c + 1) * first]
            t_fwd[there, bins:] = high[c * first:(c + 1) * first]
    sums, rest = 4 * bins, 4 * bins + PART
    high, low = split(rows(ka_row, kb_row, jnp.zeros((PART - 2, bins), F32)))
    t_fwd[sums:rest, :bins] = high
    t_fwd[sums:rest, bins:] = high
    t_fwd[rest:, :bins] = rows(al[:first], bl[:first], low)
    t_fwd[rest:, bins:] = rows(*[blank] * 5)
    t_lam[:2 * bins, :bins] = lh
    t_lam[:2 * bins, bins:] = lh
    t_lam[2 * bins:, :bins] = ll[:first]
    t_lam[2 * bins:, bins:] = rows(blank, blank)
    high, low = split(gain_ref[...])
    t_gain[:, :2 * bins] = high
    t_gain[:, 2 * bins:2 * bins + first] = high[:, :first]
    t_gain[:, 2 * bins + first:] = low[:, :first]
    lag = lag_ref[...]
    ka_col2 = jnp.concatenate([ka_col, ka_col], axis=1)
    kb_col2 = jnp.concatenate([kb_col, kb_col], axis=1)
    ah, al = split(ka_col2 * lag)
    bh, bl = split(kb_col2 * lag)
    t_lag[:, :2 * bins] = ah
    t_lag[:, 2 * bins:4 * bins] = bh
    t_lag[:, 4 * bins:] = jnp.concatenate([ah[:, :first], bh[:, :first], al[:, :first], bl[:, :first]], axis=1)

    fetches[1].wait()
    fetches[6].wait()
    wide_adj[...] = adj[...].astype(F32)
    ending = lambda x: wide_adj[pl.ds(x, bins, stride=width_x), :]

    def stencil(field, x, low_x, high_x, low_y, high_y):
        slab = field[x + 1, :bins, :]
        row = lambda k: faces[x, k:k + 1, :]
        return (
            slab * row(8)
            + row(low_x) * field[x, :bins, :]
            + row(high_x) * field[x + 2, :bins, :]
            + row(low_y) * pltpu.roll(slab, 1, 1)
            + row(high_y) * pltpu.roll(slab, width_y - 1, 1)
        )

    def packed_stencil(packed, rows_x, rows_y, low_x, high_x, low_y, high_y):
        near = pack(lambda x: faces[x], owner[:16])
        row = lambda k: near[k:k + 1]
        x_before, x_after = rows_x
        x_before = jnp.where(owner == 0, pltpu.roll(x_before, span // 2, 1), pltpu.roll(packed, span, 1))
        x_after = jnp.where(
            owner == width_x - 1, pltpu.roll(x_after, width_y - span // 2, 1), pltpu.roll(packed, width_y - span, 1))
        y_before = pltpu.roll(jnp.where(place == span // 2 - 1, rows_y[0], packed), 1, 1)
        y_after = pltpu.roll(jnp.where(place == span // 2, rows_y[1], packed), width_y - 1, 1)
        return (packed * row(8) + row(low_x) * x_before + row(high_x) * x_after
                + row(low_y) * y_before + row(high_y) * y_after)

    def coagulate(block):
        beside = lambda values: jnp.concatenate(list(values), axis=1)
        current = beside(cell[0] for cell in block)
        start = beside(cell[1] for cell in block)
        ka = beside(weights[0] for _ in block)
        kb = beside(weights[1] for _ in block)
        saved = []
        for step in range(SUBSTEPS):
            high, low = split(current)
            result = dot(t_fwd[...], rows(high, low))
            spectra = [result[c:c + corrected] for c in range(0, sums, corrected)]
            spectra[0] = spectra[0] + result[rest:rest + corrected]
            spectra = [quarters(chunk) for chunk in spectra]
            total_a, total_b = (
                result[sums + k:sums + k + 1] + result[rest + corrected + k:rest + corrected + k + 1] for k in (0, 1))
            loss = ka * total_b + kb * total_a
            saved.append((spectra, loss))
            if step < SUBSTEPS - 1:
                high, low = high_low([product(*chunk) for chunk in spectra])
                current = current + dot(t_gain[...], rows(*high, low, high[0])) - current * loss
        adjoint = start
        for step in reversed(range(SUBSTEPS)):
            spectra, loss = saved[step]
            high, low = split(adjoint)
            result = dot(t_lam[...], rows(high, low))
            spectra_l = [result[c:c + first] for c in range(0, 2 * bins, first)]
            spectra_l[0] = spectra_l[0] + result[2 * bins:]
            spectra_l = [quarters(chunk) for chunk in spectra_l]
            high_b, low_b = high_low([product_conj(*l, *v[2:]) for l, v in zip(spectra_l, spectra)])
            high_a, low_a = high_low([product_conj(*l, *v[:2]) for l, v in zip(spectra_l, spectra)])
            terms = rows(*high_b, *high_a, low_b, low_a, high_b[0], high_a[0])
            adjoint = adjoint + dot(t_lag[...], terms) - adjoint * loss
        on = beside(cell[2] for cell in block) == 1
        result = jnp.where(on, adjoint, start)
        return [result[:, index * width_y:(index + 1) * width_y] for index in range(len(block))]

    def cells_of(x):
        return stencil(state, x, 2, 5, 0, 7), ending(x), active[pl.ds(x, 1), :]

    def coagulate_rows(places):
        for x, result in zip(places, coagulate([cells_of(x) for x in places])):
            lam[x + 1] = result

    early = range(1, 1 + EARLY)
    beside_edges = range(1 + EARLY, 1 + EARLY + MIDDLE)
    late = range(1 + EARLY + MIDDLE, width_x - 1)
    packed_ending = pack(ending, owner)
    packed_active = pack(lambda x: active[pl.ds(x, 1), :], owner[:1])
    coagulate_rows(early)

    wait_y(first_y)
    for copy in first_x:
        copy.wait()
    uy_last = rows(*(unpack(y_recv[1, bins:bins + 1, :], x) for x in range(width_x)))
    by_last = rows(*(unpack(y_recv[1, bins + 1:bins + 2, :], x) for x in range(width_x)))
    uy_last = pltpu.roll(uy_last, width_y - 1, 1)
    by_last = pltpu.roll(by_last, width_y - 1, 1)
    put_faces(state[width_x + 1, bins:bins + 1, :], state[width_x + 1, bins + 1:bins + 2, :], uy_last, by_last)
    packed = packed_stencil(
        y_send[:bins, :], (state[0, :bins, :], state[width_x + 1, :bins, :]),
        (y_recv[0, :bins, :], y_recv[1, :bins, :]), 2, 5, 0, 7)
    ends = (0, width_x - 1)
    results = coagulate(
        [(packed, packed_ending, packed_active)] + [cells_of(x) for x in (*ends, *beside_edges)])
    z_send[...] = results[0]
    edge = (lane == 0) | (lane == width_y - 1)
    for x, result in zip(ends, results[1:]):
        lam[x + 1] = jnp.where(edge, unpack(results[0], x), result)
    for x, result in zip(beside_edges, results[3:]):
        lam[x + 1] = result
    second_x = x_copies(lam, 4)
    for copy in second_x:
        copy.start()
    second_y = y_copies(z_send, z_recv, 6)
    start_y(second_y, z_recv)

    coagulate_rows(late)

    wait_y(second_y)
    for copy in second_x:
        copy.wait()
    packed = packed_stencil(z_send[...], (lam[0], lam[width_x + 1]), (z_recv[0], z_recv[1]), 3, 4, 1, 6)
    near_edge = (lane < 2) | (lane >= width_y - 2)
    for x in range(width_x):
        out[pl.ds(x, bins, stride=width_x), :] = jnp.where(
            near_edge, unpack(packed, x), stencil(lam, x, 3, 4, 1, 6))


def body(n_gx, n_gy, concentration, adjoint_next, sign_x, sign_y, courant_x, courant_y, active, kernel_a, kernel_b):
    bins, width_x, width_y = concentration.shape
    cells = bins * width_x
    tables = dft_tables(bins)
    operands = (
        concentration.reshape(cells, width_y),
        adjoint_next.reshape(cells, width_y),
        sign_x, sign_y, courant_x, courant_y, active,
        kernel_a.reshape(1, bins), kernel_b.reshape(1, bins),
        *(jnp.asarray(t) for t in tables),
    )
    result = pl.pallas_call(
        functools.partial(kernel, n_gx, n_gy, width_x),
        out_shape=pltpu.VMEM((cells, width_y), F32),
        in_specs=[pl.BlockSpec(memory_space=pltpu.HBM)] * 12,
        out_specs=pl.BlockSpec(memory_space=pltpu.VMEM),
        scratch_shapes=[
            *(pltpu.VMEM(a.shape, a.dtype) for a in operands),
            pltpu.VMEM((cells, width_y), F32),
            pltpu.VMEM((cells, width_y), F32),
            pltpu.VMEM((width_x + 2, bins + 8, width_y), F32),
            pltpu.VMEM((width_x + 2, bins, width_y), F32),
            pltpu.VMEM((bins + 8, width_y), F32),
            pltpu.VMEM((2, bins + 8, width_y), F32),
            pltpu.VMEM((bins, width_y), F32),
            pltpu.VMEM((2, bins, width_y), F32),
            pltpu.VMEM((width_x, 16, width_y), F32),
            pltpu.VMEM((4 * bins + 6 * PART, 2 * bins), BF16),
            pltpu.VMEM((bins, 2 * bins + 4 * PART), BF16),
            pltpu.VMEM((2 * bins + 2 * PART, 2 * bins), BF16),
            pltpu.VMEM((bins, 4 * bins + 8 * PART), BF16),
            pltpu.VMEM((2, bins, bins), F32),
            pltpu.SemaphoreType.DMA((8,)),
            pltpu.SemaphoreType.DMA((8,)),
            pltpu.SemaphoreType.DMA((12,)),
        ],
        compiler_params=pltpu.CompilerParams(
            collective_id=0, has_side_effects=True, vmem_limit_bytes=60 * 1024 * 1024
        ),
    )(*operands)
    return result.reshape(bins, width_x, width_y)


def solution(mesh):
    return jax.shard_map(
        functools.partial(body, mesh.shape["gx"], mesh.shape["gy"]),
        mesh=mesh,
        in_specs=(
            P(None, "gx", "gy"),
            P(None, "gx", "gy"),
            P("gx", "gy"),
            P("gx", "gy"),
            P("gx", "gy"),
            P("gx", "gy"),
            P("gx", "gy"),
            P(),
            P(),
        ),
        out_specs=P(None, "gx", "gy"),
        check_vma=False,
    )
```

```python
import functools

import jax
import jax.numpy as jnp
import numpy as np
from jax import lax
from jax.experimental import pallas as pl
from jax.experimental.pallas import tpu as pltpu
from jax.sharding import PartitionSpec as P

SUBSTEPS = 4
PART = 16
BEFORE = (6,)
AFTER = (7,)
F32 = jnp.float32
BF16 = jnp.bfloat16


def dft_tables(bins):
    order = np.arange(bins)
    order = np.concatenate([order[:PART // 2], order[-(PART // 2):], order[PART // 2:-(PART // 2)]])
    freq = 2 * order + 1
    index = np.arange(bins)

    def chunked(real, imag):
        pieces = [t[c:c + PART] for c in range(0, bins, PART) for t in (real, imag)]
        return np.concatenate(pieces, axis=0)

    angle = np.pi * (freq[:, None] * index[None, :] % (4 * bins)) / (2 * bins)
    forward = chunked(np.cos(angle), -np.sin(angle))

    def inverse(outputs):
        phase = np.pi * (freq[:, None] * outputs[None, :] % (4 * bins)) / (2 * bins)
        return chunked(np.cos(phase), -np.sin(phase)).T / bins

    gain = inverse(index - 1) * (index > 0)[:, None]
    lag = inverse(index + 1) - inverse(0 * index)
    return tuple(np.asarray(t, np.float32) for t in (forward, gain, lag))


def split(values):
    high = values.astype(BF16)
    low = (values - high.astype(F32)).astype(BF16)
    return high, low


def dot(table, values):
    return jnp.dot(table, values, preferred_element_type=F32)


def rows(*values):
    return jnp.concatenate(values, axis=0)


def product(ar, ai, br, bi):
    return rows(ar * br - ai * bi, ar * bi + ai * br)


def product_conj(lr, li, vr, vi):
    return rows(lr * vr + li * vi, li * vr - lr * vi)


def quarters(chunk):
    return tuple(chunk[q * PART:(q + 1) * PART] for q in range(chunk.shape[0] // PART))


def first_precise(chunks):
    return [chunks[0], *(c.astype(BF16) for c in chunks[1:])]


def high_low(chunks):
    high, low = split(chunks[0])
    return [high, *chunks[1:]], low


def kernel(
    n_gx, n_gy, width_x,
    *refs,
):
    inputs, refs = refs[:12], refs[12:]
    out, refs = refs[0], refs[1:]
    fetched, refs = refs[:12], refs[12:]
    conc, adj, sx, sy, cx, cy, active, ka_ref, kb_ref, fwd_ref, gain_ref, lag_ref = fetched
    (wide, wide_adj, state, lam, y_send, y_recv, z_send, z_recv, own, faces, near, t_fwd, t_gain, t_lam, t_lag, weights,
     send_sem, recv_sem, in_sem) = refs
    fetches = [pltpu.make_async_copy(i, f, in_sem.at[k]) for k, (i, f) in enumerate(zip(inputs, fetched))]
    for k in (0, 2, 3, 4, 5, 1, 7, 8, 9, 10, 11, 6):
        fetches[k].start()
    bins = ka_ref.shape[1]
    width_y = sx.shape[1]
    gx = lax.axis_index("gx")
    gy = lax.axis_index("gy")
    nxt_x, prv_x = lax.rem(gx + 1, n_gx), lax.rem(gx + n_gx - 1, n_gx)
    nxt_y, prv_y = jnp.minimum(gy + 1, n_gy - 1), jnp.maximum(gy - 1, 0)
    has_prv, has_nxt = gy > 0, gy < n_gy - 1
    mesh_id = pl.DeviceIdType.MESH

    barrier = pltpu.get_barrier_semaphore()
    pl.semaphore_signal(barrier, inc=1, device_id=(prv_x, gy), device_id_type=mesh_id)
    pl.semaphore_signal(barrier, inc=1, device_id=(nxt_x, gy), device_id_type=mesh_id)

    @pl.when(has_prv)
    def _():
        pl.semaphore_signal(barrier, inc=1, device_id=(gx, prv_y), device_id_type=mesh_id)

    @pl.when(has_nxt)
    def _():
        pl.semaphore_signal(barrier, inc=1, device_id=(gx, nxt_y), device_id_type=mesh_id)

    span = width_y // width_x
    lane = lax.broadcasted_iota(jnp.int32, (bins, width_y), 1)
    owner, place = lane // span, lane % span
    lane_x = lax.broadcasted_iota(jnp.int32, (width_x, width_y), 1)
    owner_x = lane_x // span

    def pack(slab_of, owners):
        packed = slab_of(0)
        packed = pltpu.roll(packed, span // 2, 1)
        for x in range(1, width_x):
            packed = jnp.where(owners == x, pltpu.roll(slab_of(x), x * span + span // 2, 1), packed)
        return packed

    def unpack(packed, x):
        return pltpu.roll(packed, width_y - x * span - span // 2, 1)

    pieces = span // 2
    depth = bins // pieces
    shelf = ((place[:depth] + span - (pieces - 1)) % span) // 2

    def thin(packed):
        result = packed[:depth]
        for piece in range(1, pieces):
            part = pltpu.roll(packed[piece * depth:(piece + 1) * depth], 2 * piece, 1)
            result = jnp.where(shelf == piece, part, result)
        return result

    def widen(thinned):
        return rows(thinned, *(pltpu.roll(thinned, width_y - 2 * piece, 1) for piece in range(1, pieces)))

    for k in (2, 3, 4, 5):
        fetches[k].wait()
    plus_x = sx[...].astype(F32)
    plus_y = sy[...].astype(F32)
    inside = (lane_x + gy * width_y > 0).astype(F32)
    ux = cx[...] * plus_x
    bx = cx[...] * (1.0 - plus_x)
    uy = cy[...] * plus_y * inside
    by = cy[...] * (1.0 - plus_y) * inside

    def put_faces(ux_after, bx_after, uy_last, by_last):
        ux_next = rows(ux[1:], ux_after)
        bx_next = rows(bx[1:], bx_after)
        last_lane = lane_x == width_y - 1
        uy_next = jnp.where(last_lane, uy_last, pltpu.roll(uy, width_y - 1, 1))
        by_next = jnp.where(last_lane, by_last, pltpu.roll(by, width_y - 1, 1))
        centre = 1.0 - bx - ux_next - by - uy_next
        for index, values in enumerate((uy, by, ux, bx, ux_next, bx_next, uy_next, by_next, centre)):
            faces[pl.ds(index, width_x, stride=16), :] = values

    faces[...] = jnp.zeros(faces.shape, F32)
    put_faces(ux[:1], bx[:1], uy, by)

    fetches[0].wait()
    wide[...] = conc[...].astype(F32)
    for x in (0, width_x - 1):
        state[x + 1, :bins, :] = wide[pl.ds(x, bins, stride=width_x), :]
    state[1, bins:bins + 1, :] = ux[0:1]
    state[1, bins + 1:bins + 2, :] = bx[0:1]
    state[1, bins + 2:, :] = jnp.zeros((6, width_y), F32)
    state[width_x, bins:, :] = jnp.zeros((8, width_y), F32)

    def x_copies(field, base):
        return (
            pltpu.make_async_remote_copy(
                src_ref=field.at[1], dst_ref=field.at[width_x + 1],
                send_sem=send_sem.at[base], recv_sem=recv_sem.at[base],
                device_id=(prv_x, gy), device_id_type=mesh_id),
            pltpu.make_async_remote_copy(
                src_ref=field.at[width_x], dst_ref=field.at[0],
                send_sem=send_sem.at[base + 1], recv_sem=recv_sem.at[base + 1],
                device_id=(nxt_x, gy), device_id_type=mesh_id),
        )

    pl.semaphore_wait(barrier, 2 + has_prv.astype(jnp.int32) + has_nxt.astype(jnp.int32))
    first_x = x_copies(state, 0)
    for copy in first_x:
        copy.start()
    for x in range(1, width_x - 1):
        state[x + 1, :bins, :] = wide[pl.ds(x, bins, stride=width_x), :]

    packed = pack(lambda x: state[x + 1, :bins, :], owner)
    own[...] = packed
    y_send[:depth, :] = thin(packed)
    y_send[depth:, :] = pack(lambda x: faces[x * 16:x * 16 + 8, :], owner[:8])

    def y_copies(source, target, base):
        return (
            pltpu.make_async_remote_copy(
                src_ref=source, dst_ref=target.at[1],
                send_sem=send_sem.at[base], recv_sem=recv_sem.at[base],
                device_id=(gx, prv_y), device_id_type=mesh_id),
            pltpu.make_async_remote_copy(
                src_ref=source, dst_ref=target.at[0],
                send_sem=send_sem.at[base + 1], recv_sem=recv_sem.at[base + 1],
                device_id=(gx, nxt_y), device_id_type=mesh_id),
        )

    def start_y(copies, target):
        to_prv, to_nxt = copies

        @pl.when(has_prv)
        def _():
            to_prv.start()

        @pl.when(has_nxt)
        def _():
            to_nxt.start()

        @pl.when(jnp.logical_not(has_prv))
        def _():
            target[0] = jnp.zeros(target.shape[1:], F32)

        @pl.when(jnp.logical_not(has_nxt))
        def _():
            target[1] = jnp.zeros(target.shape[1:], F32)

    def wait_y(copies):
        to_prv, to_nxt = copies

        @pl.when(has_prv)
        def _():
            to_prv.wait_send()
            to_nxt.wait_recv()

        @pl.when(has_nxt)
        def _():
            to_nxt.wait_send()
            to_prv.wait_recv()

    first_y = y_copies(y_send, y_recv, 2)
    start_y(first_y, y_recv)

    for k in (7, 8, 9, 10, 11):
        fetches[k].wait()
    ka_row, kb_row = ka_ref[...], kb_ref[...]
    weights[0] = jnp.broadcast_to(ka_row, (bins, bins)).T
    weights[1] = jnp.broadcast_to(kb_row, (bins, bins)).T
    ka_col, kb_col = weights[0], weights[1]
    first, corrected = 2 * PART, 4 * PART
    forward = fwd_ref[...]
    ah, al = split(forward * ka_row)
    bh, bl = split(forward * kb_row)
    lh, ll = split(forward)
    blank = jnp.zeros((PART, bins), BF16)
    for c in range(bins // PART):
        for q, high in enumerate((ah, bh)):
            there = slice(c * corrected + q * first, c * corrected + (q + 1) * first)
            t_fwd[there, :bins] = high[c * first:(c + 1) * first]
            t_fwd[there, bins:] = high[c * first:(c + 1) * first]
    sums, rest = 4 * bins, 4 * bins + PART
    high, low = split(rows(ka_row, kb_row, jnp.zeros((PART - 2, bins), F32)))
    t_fwd[sums:rest, :bins] = high
    t_fwd[sums:rest, bins:] = high
    t_fwd[rest:, :bins] = rows(al[:first], bl[:first], low)
    t_fwd[rest:, bins:] = rows(*[blank] * 5)
    t_lam[:2 * bins, :bins] = lh
    t_lam[:2 * bins, bins:] = lh
    t_lam[2 * bins:, :bins] = ll[:first]
    t_lam[2 * bins:, bins:] = rows(blank, blank)
    high, low = split(gain_ref[...])
    t_gain[:, :2 * bins] = high
    t_gain[:, 2 * bins:2 * bins + first] = high[:, :first]
    t_gain[:, 2 * bins + first:] = low[:, :first]
    lag = lag_ref[...]
    ka_col2 = jnp.concatenate([ka_col, ka_col], axis=1)
    kb_col2 = jnp.concatenate([kb_col, kb_col], axis=1)
    ah, al = split(ka_col2 * lag)
    bh, bl = split(kb_col2 * lag)
    t_lag[:, :2 * bins] = ah
    t_lag[:, 2 * bins:4 * bins] = bh
    t_lag[:, 4 * bins:] = jnp.concatenate([ah[:, :first], bh[:, :first], al[:, :first], bl[:, :first]], axis=1)

    fetches[1].wait()
    fetches[6].wait()
    wide_adj[...] = adj[...].astype(F32)
    ending = lambda x: wide_adj[pl.ds(x, bins, stride=width_x), :]

    def stencil(field, x, low_x, high_x, low_y, high_y):
        slab = field[x + 1, :bins, :]
        row = lambda k: faces[x * 16 + k:x * 16 + k + 1, :]
        return (
            slab * row(8)
            + row(low_x) * field[x, :bins, :]
            + row(high_x) * field[x + 2, :bins, :]
            + row(low_y) * pltpu.roll(slab, 1, 1)
            + row(high_y) * pltpu.roll(slab, width_y - 1, 1)
        )

    def packed_stencil(packed, rows_x, rows_y, low_x, high_x, low_y, high_y):
        row = lambda k: near[k:k + 1, :]
        x_before, x_after = rows_x
        x_before = jnp.where(owner == 0, pltpu.roll(x_before, span // 2, 1), pltpu.roll(packed, span, 1))
        x_after = jnp.where(
            owner == width_x - 1, pltpu.roll(x_after, width_y - span // 2, 1), pltpu.roll(packed, width_y - span, 1))
        y_before = pltpu.roll(jnp.where(place == span // 2 - 1, rows_y[0], packed), 1, 1)
        y_after = pltpu.roll(jnp.where(place == span // 2, rows_y[1], packed), width_y - 1, 1)
        return (packed * row(8) + row(low_x) * x_before + row(high_x) * x_after
                + row(low_y) * y_before + row(high_y) * y_after)

    def beside(values):
        return jnp.concatenate(list(values), axis=1)

    def forward_steps(block, saved):
        current = beside(cell[0] for cell in block)
        ka = beside(weights[0] for _ in block)
        kb = beside(weights[1] for _ in block)
        for step in range(SUBSTEPS):
            high, low = split(current)
            result = dot(t_fwd[...], rows(high, low))
            yield
            spectra = [result[c:c + corrected] for c in range(0, sums, corrected)]
            spectra[0] = spectra[0] + result[rest:rest + corrected]
            spectra = [quarters(chunk) for chunk in first_precise(spectra)]
            total_a, total_b = (
                result[sums + k:sums + k + 1] + result[rest + corrected + k:rest + corrected + k + 1] for k in (0, 1))
            loss = ka * total_b + kb * total_a
            saved.append((spectra, loss))
            if step < SUBSTEPS - 1:
                high, low = high_low([product(*chunk) for chunk in spectra])
                current = current + dot(t_gain[...], rows(*high, low, high[0])) - current * loss
            yield

    def backward_steps(block, saved, results):
        start = beside(cell[1] for cell in block)
        adjoint = start
        for spectra, loss in reversed(saved):
            high, low = split(adjoint)
            result = dot(t_lam[...], rows(high, low))
            yield
            spectra_l = [result[c:c + first] for c in range(0, 2 * bins, first)]
            spectra_l[0] = spectra_l[0] + result[2 * bins:]
            spectra_l = [quarters(chunk) for chunk in first_precise(spectra_l)]
            high_b, low_b = high_low([product_conj(*l, *v[2:]) for l, v in zip(spectra_l, spectra)])
            high_a, low_a = high_low([product_conj(*l, *v[:2]) for l, v in zip(spectra_l, spectra)])
            terms = rows(*high_b, *high_a, low_b, low_a, high_b[0], high_a[0])
            adjoint = adjoint + dot(t_lag[...], terms) - adjoint * loss
            yield
        on = beside(cell[2] for cell in block) == 1
        result = jnp.where(on, adjoint, start)
        results += [result[:, index * width_y:(index + 1) * width_y] for index in range(len(block))]

    def run(*phases):
        phases = list(phases)
        while phases:
            phases = [phase for phase in phases if next(phase, phases) is None]

    def cells_of(x):
        return stencil(state, x, 2, 5, 0, 7), ending(x), active[pl.ds(x, 1), :]

    class Group:
        def __init__(self, places, extra=()):
            self.places = places
            self.cells = [*extra, *(cells_of(x) for x in places)]
            self.saved, self.results = [], []

        def forward(self):
            return forward_steps(self.cells, self.saved)

        def backward(self):
            return backward_steps(self.cells, self.saved, self.results)

        def put(self):
            for x, result in zip(self.places, self.results):
                lam[x + 1] = result

    inner = iter(range(1, width_x - 1))
    take = lambda count: [next(inner) for _ in range(count)]
    ends = (0, width_x - 1)
    previous = Group(take(BEFORE[0]))
    run(previous.forward())
    for count in BEFORE[1:]:
        group = Group(take(count))
        run(previous.backward(), group.forward())
        previous.put()
        previous = group
    packed_ending = pack(ending, owner)
    packed_active = pack(lambda x: active[pl.ds(x, 1), :], owner[:1])

    wait_y(first_y)
    for copy in first_x:
        copy.wait()
    uy_last = rows(*(unpack(y_recv[1, depth:depth + 1, :], x) for x in range(width_x)))
    by_last = rows(*(unpack(y_recv[1, depth + 1:depth + 2, :], x) for x in range(width_x)))
    uy_last = pltpu.roll(uy_last, width_y - 1, 1)
    by_last = pltpu.roll(by_last, width_y - 1, 1)
    put_faces(state[width_x + 1, bins:bins + 1, :], state[width_x + 1, bins + 1:bins + 2, :], uy_last, by_last)
    near[...] = pack(lambda x: faces[x * 16:(x + 1) * 16, :], owner[:16])
    packed = packed_stencil(
        own[...], (state[0, :bins, :], state[width_x + 1, :bins, :]),
        (widen(y_recv[0, :depth, :]), widen(y_recv[1, :depth, :])), 2, 5, 0, 7)
    edges = Group([*ends, *take(width_x - 2 - sum(BEFORE) - sum(AFTER))], [(packed, packed_ending, packed_active)])
    run(previous.backward(), edges.forward())
    previous.put()
    previous = Group(take(AFTER[0]))
    run(edges.backward(), previous.forward())
    packed, *edges.results = edges.results
    own[...] = packed
    z_send[...] = thin(packed)
    edge = (lane == 0) | (lane == width_y - 1)
    for k, x in enumerate(ends):
        edges.results[k] = jnp.where(edge, unpack(packed, x), edges.results[k])
    edges.put()
    second_x = x_copies(lam, 4)
    for copy in second_x:
        copy.start()
    second_y = y_copies(z_send, z_recv, 6)
    start_y(second_y, z_recv)

    for count in AFTER[1:]:
        group = Group(take(count))
        run(previous.backward(), group.forward())
        previous.put()
        previous = group
    run(previous.backward())
    previous.put()
    for x in range(1, width_x - 1):
        wide[x * bins:(x + 1) * bins, :] = stencil(lam, x, 3, 4, 1, 6)

    wait_y(second_y)
    for copy in second_x:
        copy.wait()
    for x in ends:
        wide[x * bins:(x + 1) * bins, :] = stencil(lam, x, 3, 4, 1, 6)
    packed = packed_stencil(
        own[...], (lam[0], lam[width_x + 1]), (widen(z_recv[0]), widen(z_recv[1])), 3, 4, 1, 6)
    near_edge = (lane < 2) | (lane >= width_y - 2)
    for x in range(width_x):
        out[pl.ds(x, bins, stride=width_x), :] = jnp.where(
            near_edge, unpack(packed, x), wide[x * bins:(x + 1) * bins, :])


def body(n_gx, n_gy, concentration, adjoint_next, sign_x, sign_y, courant_x, courant_y, active, kernel_a, kernel_b):
    bins, width_x, width_y = concentration.shape
    cells = bins * width_x
    depth = bins * 2 * width_x // width_y
    tables = dft_tables(bins)
    operands = (
        concentration.reshape(cells, width_y),
        adjoint_next.reshape(cells, width_y),
        sign_x, sign_y, courant_x, courant_y, active,
        kernel_a.reshape(1, bins), kernel_b.reshape(1, bins),
        *(jnp.asarray(t) for t in tables),
    )
    result = pl.pallas_call(
        functools.partial(kernel, n_gx, n_gy, width_x),
        out_shape=pltpu.VMEM((cells, width_y), F32),
        in_specs=[pl.BlockSpec(memory_space=pltpu.HBM)] * 12,
        out_specs=pl.BlockSpec(memory_space=pltpu.VMEM),
        scratch_shapes=[
            *(pltpu.VMEM(a.shape, a.dtype) for a in operands),
            pltpu.VMEM((cells, width_y), F32),
            pltpu.VMEM((cells, width_y), F32),
            pltpu.VMEM((width_x + 2, bins + 8, width_y), F32),
            pltpu.VMEM((width_x + 2, bins, width_y), F32),
            pltpu.VMEM((depth + 8, width_y), F32),
            pltpu.VMEM((2, depth + 8, width_y), F32),
            pltpu.VMEM((depth, width_y), F32),
            pltpu.VMEM((2, depth, width_y), F32),
            pltpu.VMEM((bins, width_y), F32),
            pltpu.VMEM((16 * width_x, width_y), F32),
            pltpu.VMEM((16, width_y), F32),
            pltpu.VMEM((4 * bins + 6 * PART, 2 * bins), BF16),
            pltpu.VMEM((bins, 2 * bins + 4 * PART), BF16),
            pltpu.VMEM((2 * bins + 2 * PART, 2 * bins), BF16),
            pltpu.VMEM((bins, 4 * bins + 8 * PART), BF16),
            pltpu.VMEM((2, bins, bins), F32),
            pltpu.SemaphoreType.DMA((8,)),
            pltpu.SemaphoreType.DMA((8,)),
            pltpu.SemaphoreType.DMA((12,)),
        ],
        compiler_params=pltpu.CompilerParams(
            collective_id=0, has_side_effects=True, vmem_limit_bytes=60 * 1024 * 1024
        ),
    )(*operands)
    return result.reshape(bins, width_x, width_y)


def solution(mesh):
    return jax.shard_map(
        functools.partial(body, mesh.shape["gx"], mesh.shape["gy"]),
        mesh=mesh,
        in_specs=(
            P(None, "gx", "gy"),
            P(None, "gx", "gy"),
            P("gx", "gy"),
            P("gx", "gy"),
            P("gx", "gy"),
            P("gx", "gy"),
            P("gx", "gy"),
            P(),
            P(),
        ),
        out_specs=P(None, "gx", "gy"),
        check_vma=False,
    )
```

```python
import functools

import jax
import jax.numpy as jnp
import numpy as np
from jax import lax
from jax.experimental import pallas as pl
from jax.experimental.pallas import tpu as pltpu
from jax.sharding import PartitionSpec as P

SUBSTEPS = 4
PART = 16
BEFORE = 8
AFTER = 6
LEAD = 2
BESIDE = 4
F32 = jnp.float32
BF16 = jnp.bfloat16


def dft_tables(bins):
    order = np.arange(bins)
    order = np.concatenate([order[:PART // 2], order[-(PART // 2):], order[PART // 2:-(PART // 2)]])
    freq = 2 * order + 1
    index = np.arange(bins)

    def chunked(real, imag):
        pieces = [t[c:c + PART] for c in range(0, bins, PART) for t in (real, imag)]
        return np.concatenate(pieces, axis=0)

    angle = np.pi * (freq[:, None] * index[None, :] % (4 * bins)) / (2 * bins)
    forward = chunked(np.cos(angle), -np.sin(angle))

    def inverse(outputs):
        phase = np.pi * (freq[:, None] * outputs[None, :] % (4 * bins)) / (2 * bins)
        return chunked(np.cos(phase), -np.sin(phase)).T / bins

    gain = inverse(index - 1) * (index > 0)[:, None]
    lag = inverse(index + 1) - inverse(0 * index)
    return tuple(np.asarray(t, np.float32) for t in (forward, gain, lag))


def split(values):
    high = values.astype(BF16)
    low = (values - high.astype(F32)).astype(BF16)
    return high, low


def dot(table, values):
    return jnp.dot(table, values, preferred_element_type=F32)


def rows(*values):
    return jnp.concatenate(values, axis=0)


def product(ar, ai, br, bi):
    return rows(ar * br - ai * bi, ar * bi + ai * br)


def product_conj(lr, li, vr, vi):
    return rows(lr * vr + li * vi, li * vr - lr * vi)


def quarters(chunk):
    return tuple(chunk[q * PART:(q + 1) * PART] for q in range(chunk.shape[0] // PART))


def first_precise(chunks):
    return [chunks[0], *(c.astype(BF16) for c in chunks[1:])]


def high_low(chunks):
    high, low = split(chunks[0])
    return [high, *chunks[1:]], low


def kernel(
    n_gx, n_gy, width_x,
    *refs,
):
    inputs, refs = refs[:12], refs[12:]
    out, refs = refs[0], refs[1:]
    fetched, refs = refs[:12], refs[12:]
    conc, adj, sx, sy, cx, cy, active, ka_ref, kb_ref, fwd_ref, gain_ref, lag_ref = fetched
    (wide, wide_adj, state, lam, y_send, y_recv, z_send, z_recv, own, faces, near, t_fwd, t_gain, t_lam, t_lag, weights,
     send_sem, recv_sem, in_sem) = refs
    fetches = [pltpu.make_async_copy(i, f, in_sem.at[k]) for k, (i, f) in enumerate(zip(inputs, fetched))]
    for k in (0, 2, 3, 4, 5, 1, 7, 8, 9, 10, 11, 6):
        fetches[k].start()
    bins = ka_ref.shape[1]
    width_y = sx.shape[1]
    gx = lax.axis_index("gx")
    gy = lax.axis_index("gy")
    nxt_x, prv_x = lax.rem(gx + 1, n_gx), lax.rem(gx + n_gx - 1, n_gx)
    nxt_y, prv_y = jnp.minimum(gy + 1, n_gy - 1), jnp.maximum(gy - 1, 0)
    has_prv, has_nxt = gy > 0, gy < n_gy - 1
    mesh_id = pl.DeviceIdType.MESH

    barrier = pltpu.get_barrier_semaphore()
    pl.semaphore_signal(barrier, inc=1, device_id=(prv_x, gy), device_id_type=mesh_id)
    pl.semaphore_signal(barrier, inc=1, device_id=(nxt_x, gy), device_id_type=mesh_id)

    @pl.when(has_prv)
    def _():
        pl.semaphore_signal(barrier, inc=1, device_id=(gx, prv_y), device_id_type=mesh_id)

    @pl.when(has_nxt)
    def _():
        pl.semaphore_signal(barrier, inc=1, device_id=(gx, nxt_y), device_id_type=mesh_id)

    span = width_y // width_x
    lane = lax.broadcasted_iota(jnp.int32, (bins, width_y), 1)
    owner, place = lane // span, lane % span
    lane_x = lax.broadcasted_iota(jnp.int32, (width_x, width_y), 1)
    owner_x = lane_x // span

    def shift_of(x):
        return (width_x - 1 - x) * span + span // 2

    def pack_steps(slab_of, owners, results):
        packed = pltpu.roll(slab_of(width_x - 1), span // 2, 1)
        for x in range(width_x - 1):
            packed = jnp.where(owners == width_x - 1 - x, pltpu.roll(slab_of(x), shift_of(x), 1), packed)
            if x % 2:
                yield
        results.append(packed)

    def pack(slab_of, owners):
        results = []
        run(pack_steps(slab_of, owners, results))
        return results[0]

    def unpack(packed, x):
        return pltpu.roll(packed, width_y - shift_of(x), 1)

    def run(steps, count=None):
        if count is None:
            for _ in steps:
                pass
        else:
            for _ in range(count):
                next(steps, None)

    def weave(steps, others, count):
        total = 2 * SUBSTEPS
        for index, _ in enumerate(steps):
            run(others, (index + 1) * count // total - index * count // total)

    pieces = span // 2
    depth = bins // pieces
    shelf = ((place[:depth] + span - (pieces - 1)) % span) // 2

    def thin(packed):
        result = packed[:depth]
        for piece in range(1, pieces):
            part = pltpu.roll(packed[piece * depth:(piece + 1) * depth], 2 * piece, 1)
            result = jnp.where(shelf == piece, part, result)
        return result

    def widen(thinned):
        return rows(thinned, *(pltpu.roll(thinned, width_y - 2 * piece, 1) for piece in range(1, pieces)))

    for k in (2, 3, 4, 5):
        fetches[k].wait()
    plus_x = sx[...].astype(F32)
    plus_y = sy[...].astype(F32)
    inside = (lane_x + gy * width_y > 0).astype(F32)
    ux = cx[...] * plus_x
    bx = cx[...] * (1.0 - plus_x)
    uy = cy[...] * plus_y * inside
    by = cy[...] * (1.0 - plus_y) * inside

    def put_faces(ux_after, bx_after, uy_last, by_last):
        ux_next = rows(ux[1:], ux_after)
        bx_next = rows(bx[1:], bx_after)
        last_lane = lane_x == width_y - 1
        uy_next = jnp.where(last_lane, uy_last, pltpu.roll(uy, width_y - 1, 1))
        by_next = jnp.where(last_lane, by_last, pltpu.roll(by, width_y - 1, 1))
        centre = 1.0 - bx - ux_next - by - uy_next
        for index, values in enumerate((uy, by, ux, bx, ux_next, bx_next, uy_next, by_next, centre)):
            faces[pl.ds(index, width_x, stride=16), :] = values

    faces[...] = jnp.zeros(faces.shape, F32)
    put_faces(ux[:1], bx[:1], uy, by)

    fetches[0].wait()
    wide[...] = conc[...].astype(F32)
    for x in (0, width_x - 1):
        state[x + 1, :bins, :] = wide[pl.ds(x, bins, stride=width_x), :]
    state[1, bins:bins + 1, :] = ux[0:1]
    state[1, bins + 1:bins + 2, :] = bx[0:1]
    state[1, bins + 2:, :] = jnp.zeros((6, width_y), F32)
    state[width_x, bins:, :] = jnp.zeros((8, width_y), F32)

    def x_copies(field, base):
        return (
            pltpu.make_async_remote_copy(
                src_ref=field.at[1], dst_ref=field.at[width_x + 1],
                send_sem=send_sem.at[base], recv_sem=recv_sem.at[base],
                device_id=(prv_x, gy), device_id_type=mesh_id),
            pltpu.make_async_remote_copy(
                src_ref=field.at[width_x], dst_ref=field.at[0],
                send_sem=send_sem.at[base + 1], recv_sem=recv_sem.at[base + 1],
                device_id=(nxt_x, gy), device_id_type=mesh_id),
        )

    pl.semaphore_wait(barrier, 2 + has_prv.astype(jnp.int32) + has_nxt.astype(jnp.int32))
    first_x = x_copies(state, 0)
    for copy in first_x:
        copy.start()
    for x in range(1, width_x - 1):
        state[x + 1, :bins, :] = wide[pl.ds(x, bins, stride=width_x), :]

    packed = pack(lambda x: state[x + 1, :bins, :], owner)
    own[...] = packed
    y_send[:depth, :] = thin(packed)
    y_send[depth:, :] = pack(lambda x: faces[x * 16:x * 16 + 8, :], owner[:8])

    def y_copies(source, target, base):
        return (
            pltpu.make_async_remote_copy(
                src_ref=source, dst_ref=target.at[1],
                send_sem=send_sem.at[base], recv_sem=recv_sem.at[base],
                device_id=(gx, prv_y), device_id_type=mesh_id),
            pltpu.make_async_remote_copy(
                src_ref=source, dst_ref=target.at[0],
                send_sem=send_sem.at[base + 1], recv_sem=recv_sem.at[base + 1],
                device_id=(gx, nxt_y), device_id_type=mesh_id),
        )

    def start_y(copies, target):
        to_prv, to_nxt = copies

        @pl.when(has_prv)
        def _():
            to_prv.start()

        @pl.when(has_nxt)
        def _():
            to_nxt.start()

        @pl.when(jnp.logical_not(has_prv))
        def _():
            target[0] = jnp.zeros(target.shape[1:], F32)

        @pl.when(jnp.logical_not(has_nxt))
        def _():
            target[1] = jnp.zeros(target.shape[1:], F32)

    def wait_y(copies):
        to_prv, to_nxt = copies

        @pl.when(has_prv)
        def _():
            to_prv.wait_send()
            to_nxt.wait_recv()

        @pl.when(has_nxt)
        def _():
            to_nxt.wait_send()
            to_prv.wait_recv()

    first_y = y_copies(y_send, y_recv, 2)
    start_y(first_y, y_recv)

    for k in (7, 8, 9, 10, 11):
        fetches[k].wait()
    ka_row, kb_row = ka_ref[...], kb_ref[...]
    weights[0] = jnp.broadcast_to(ka_row, (bins, bins)).T
    weights[1] = jnp.broadcast_to(kb_row, (bins, bins)).T
    ka_col, kb_col = weights[0], weights[1]
    first, corrected = 2 * PART, 4 * PART
    forward = fwd_ref[...]
    ah, al = split(forward * ka_row)
    bh, bl = split(forward * kb_row)
    lh, ll = split(forward)
    blank = jnp.zeros((PART, bins), BF16)
    for c in range(bins // PART):
        for q, high in enumerate((ah, bh)):
            there = slice(c * corrected + q * first, c * corrected + (q + 1) * first)
            t_fwd[there, :bins] = high[c * first:(c + 1) * first]
            t_fwd[there, bins:] = high[c * first:(c + 1) * first]
    sums, rest = 4 * bins, 4 * bins + PART
    high, low = split(rows(ka_row, kb_row, jnp.zeros((PART - 2, bins), F32)))
    t_fwd[sums:rest, :bins] = high
    t_fwd[sums:rest, bins:] = high
    t_fwd[rest:, :bins] = rows(al[:first], bl[:first], low)
    t_fwd[rest:, bins:] = rows(*[blank] * 5)
    t_lam[:2 * bins, :bins] = lh
    t_lam[:2 * bins, bins:] = lh
    t_lam[2 * bins:, :bins] = ll[:first]
    t_lam[2 * bins:, bins:] = rows(blank, blank)
    high, low = split(gain_ref[...])
    t_gain[:, :2 * bins] = high
    t_gain[:, 2 * bins:2 * bins + first] = high[:, :first]
    t_gain[:, 2 * bins + first:] = low[:, :first]
    lag = lag_ref[...]
    ka_col2 = jnp.concatenate([ka_col, ka_col], axis=1)
    kb_col2 = jnp.concatenate([kb_col, kb_col], axis=1)
    ah, al = split(ka_col2 * lag)
    bh, bl = split(kb_col2 * lag)
    t_lag[:, :2 * bins] = ah
    t_lag[:, 2 * bins:4 * bins] = bh
    t_lag[:, 4 * bins:] = jnp.concatenate([ah[:, :first], bh[:, :first], al[:, :first], bl[:, :first]], axis=1)

    fetches[1].wait()
    fetches[6].wait()
    wide_adj[...] = adj[...].astype(F32)
    ending = lambda x: wide_adj[pl.ds(x, bins, stride=width_x), :]

    def stencil(field, x, low_x, high_x, low_y, high_y):
        slab = field[x + 1, :bins, :]
        row = lambda k: faces[x * 16 + k:x * 16 + k + 1, :]
        return (
            slab * row(8)
            + row(low_x) * field[x, :bins, :]
            + row(high_x) * field[x + 2, :bins, :]
            + row(low_y) * pltpu.roll(slab, 1, 1)
            + row(high_y) * pltpu.roll(slab, width_y - 1, 1)
        )

    def packed_stencil(packed, rows_x, rows_y, low_x, high_x, low_y, high_y):
        row = lambda k: near[k:k + 1, :]
        x_before, x_after = rows_x
        x_before = jnp.where(
            owner == width_x - 1, pltpu.roll(x_before, width_y - span // 2, 1), pltpu.roll(packed, width_y - span, 1))
        x_after = jnp.where(owner == 0, pltpu.roll(x_after, span // 2, 1), pltpu.roll(packed, span, 1))
        y_before = pltpu.roll(jnp.where(place == span // 2 - 1, rows_y[0], packed), 1, 1)
        y_after = pltpu.roll(jnp.where(place == span // 2, rows_y[1], packed), width_y - 1, 1)
        return (packed * row(8) + row(low_x) * x_before + row(high_x) * x_after
                + row(low_y) * y_before + row(high_y) * y_after)

    def beside(values):
        return jnp.concatenate(list(values), axis=1)

    def forward_steps(block, saved):
        current = beside(cell[0] for cell in block)
        ka = beside(weights[0] for _ in block)
        kb = beside(weights[1] for _ in block)
        for step in range(SUBSTEPS):
            high, low = split(current)
            result = dot(t_fwd[...], rows(high, low))
            yield
            spectra = [result[c:c + corrected] for c in range(0, sums, corrected)]
            spectra[0] = spectra[0] + result[rest:rest + corrected]
            spectra = [quarters(chunk) for chunk in first_precise(spectra)]
            total_a, total_b = (
                result[sums + k:sums + k + 1] + result[rest + corrected + k:rest + corrected + k + 1] for k in (0, 1))
            loss = ka * total_b + kb * total_a
            saved.append((spectra, loss))
            if step < SUBSTEPS - 1:
                high, low = high_low([product(*chunk) for chunk in spectra])
                current = current + dot(t_gain[...], rows(*high, low, high[0])) - current * loss
            yield

    def backward_steps(block, saved, results):
        start = beside(cell[1] for cell in block)
        adjoint = start
        for spectra, loss in reversed(saved):
            high, low = split(adjoint)
            result = dot(t_lam[...], rows(high, low))
            yield
            spectra_l = [result[c:c + first] for c in range(0, 2 * bins, first)]
            spectra_l[0] = spectra_l[0] + result[2 * bins:]
            spectra_l = [quarters(chunk) for chunk in first_precise(spectra_l)]
            high_b, low_b = high_low([product_conj(*l, *v[2:]) for l, v in zip(spectra_l, spectra)])
            high_a, low_a = high_low([product_conj(*l, *v[:2]) for l, v in zip(spectra_l, spectra)])
            terms = rows(*high_b, *high_a, low_b, low_a, high_b[0], high_a[0])
            adjoint = adjoint + dot(t_lag[...], terms) - adjoint * loss
            yield
        on = beside(cell[2] for cell in block) == 1
        result = jnp.where(on, adjoint, start)
        results += [result[:, index * width_y:(index + 1) * width_y] for index in range(len(block))]

    def cells_of(x):
        return stencil(state, x, 2, 5, 0, 7), ending(x), active[pl.ds(x, 1), :]

    class Group:
        def __init__(self, places, cells):
            self.places, self.cells = places, cells
            self.saved, self.results = [], []

        def forward(self):
            return forward_steps(self.cells, self.saved)

        def backward(self):
            return backward_steps(self.cells, self.saved, self.results)

        def put(self):
            for x, result in zip(self.places, self.results):
                lam[x + 1] = result

    inner = iter(range(1, width_x - 1))
    take = lambda count: [next(inner) for _ in range(count)]
    ends = (0, width_x - 1)
    places = take(BEFORE)
    early = Group(places, [cells_of(x) for x in places])
    middle_places = [*ends, *take(width_x - 2 - BEFORE - AFTER)]
    late = Group(take(AFTER), [])
    packed_ending = []

    def prepare():
        yield from pack_steps(ending, owner, packed_ending)
        for x in late.places:
            late.cells.append(cells_of(x))
            yield

    preparing = prepare()
    weave(early.forward(), preparing, width_x // 2 + AFTER)
    run(preparing)
    packed_active = pack(lambda x: active[pl.ds(x, 1), :], owner[:1])
    early_steps = early.backward()
    run(early_steps, LEAD)

    wait_y(first_y)
    for copy in first_x:
        copy.wait()
    uy_last = rows(*(unpack(y_recv[1, depth:depth + 1, :], x) for x in range(width_x)))
    by_last = rows(*(unpack(y_recv[1, depth + 1:depth + 2, :], x) for x in range(width_x)))
    uy_last = pltpu.roll(uy_last, width_y - 1, 1)
    by_last = pltpu.roll(by_last, width_y - 1, 1)
    put_faces(state[width_x + 1, bins:bins + 1, :], state[width_x + 1, bins + 1:bins + 2, :], uy_last, by_last)
    near[...] = pack(lambda x: faces[x * 16:(x + 1) * 16, :], owner[:16])
    packed = packed_stencil(
        own[...], (state[0, :bins, :], state[width_x + 1, :bins, :]),
        (widen(y_recv[0, :depth, :]), widen(y_recv[1, :depth, :])), 2, 5, 0, 7)
    edges = Group(
        middle_places, [(packed, packed_ending[0], packed_active)] + [cells_of(x) for x in middle_places])
    weave(edges.forward(), early_steps, 2 * SUBSTEPS - LEAD)
    run(early_steps)
    early.put()
    late_steps = late.forward()
    weave(edges.backward(), late_steps, BESIDE)
    packed, *edges.results = edges.results
    own[...] = packed
    z_send[...] = thin(packed)
    edge = (lane == 0) | (lane == width_y - 1)
    for k, x in enumerate(ends):
        edges.results[k] = jnp.where(edge, unpack(packed, x), edges.results[k])
    edges.put()
    second_x = x_copies(lam, 4)
    for copy in second_x:
        copy.start()
    second_y = y_copies(z_send, z_recv, 6)
    start_y(second_y, z_recv)

    def finish(places):
        for x in places:
            out[pl.ds(x, bins, stride=width_x), :] = stencil(lam, x, 3, 4, 1, 6)
            yield

    run(late_steps)
    weave(late.backward(), finish(range(1, BEFORE)), BEFORE - 1)
    late.put()
    run(finish(range(BEFORE, width_x - 1)))

    wait_y(second_y)
    for copy in second_x:
        copy.wait()
    run(finish(ends))
    packed = packed_stencil(
        own[...], (lam[0], lam[width_x + 1]), (widen(z_recv[0]), widen(z_recv[1])), 3, 4, 1, 6)
    own[...] = packed
    near_edge = ((lane < 2) | (lane >= width_y - 2))[:8]
    for b in range(bins):
        for x in range(0, width_x, 8):
            here = slice(b * width_x + x, b * width_x + x + 8)
            cells = jnp.broadcast_to(own[b:b + 1, :], (8, width_y))
            cells = pltpu.roll(cells, width_y - shift_of(x), 1, stride=span, stride_axis=0)
            out[here, :] = jnp.where(near_edge, cells, out[here, :])


def body(n_gx, n_gy, concentration, adjoint_next, sign_x, sign_y, courant_x, courant_y, active, kernel_a, kernel_b):
    bins, width_x, width_y = concentration.shape
    cells = bins * width_x
    depth = bins * 2 * width_x // width_y
    tables = dft_tables(bins)
    operands = (
        concentration.reshape(cells, width_y),
        adjoint_next.reshape(cells, width_y),
        sign_x, sign_y, courant_x, courant_y, active,
        kernel_a.reshape(1, bins), kernel_b.reshape(1, bins),
        *(jnp.asarray(t) for t in tables),
    )
    result = pl.pallas_call(
        functools.partial(kernel, n_gx, n_gy, width_x),
        out_shape=pltpu.VMEM((cells, width_y), F32),
        in_specs=[pl.BlockSpec(memory_space=pltpu.HBM)] * 12,
        out_specs=pl.BlockSpec(memory_space=pltpu.VMEM),
        scratch_shapes=[
            *(pltpu.VMEM(a.shape, a.dtype) for a in operands),
            pltpu.VMEM((cells, width_y), F32),
            pltpu.VMEM((cells, width_y), F32),
            pltpu.VMEM((width_x + 2, bins + 8, width_y), F32),
            pltpu.VMEM((width_x + 2, bins, width_y), F32),
            pltpu.VMEM((depth + 8, width_y), F32),
            pltpu.VMEM((2, depth + 8, width_y), F32),
            pltpu.VMEM((depth, width_y), F32),
            pltpu.VMEM((2, depth, width_y), F32),
            pltpu.VMEM((bins, width_y), F32),
            pltpu.VMEM((16 * width_x, width_y), F32),
            pltpu.VMEM((16, width_y), F32),
            pltpu.VMEM((4 * bins + 6 * PART, 2 * bins), BF16),
            pltpu.VMEM((bins, 2 * bins + 4 * PART), BF16),
            pltpu.VMEM((2 * bins + 2 * PART, 2 * bins), BF16),
            pltpu.VMEM((bins, 4 * bins + 8 * PART), BF16),
            pltpu.VMEM((2, bins, bins), F32),
            pltpu.SemaphoreType.DMA((8,)),
            pltpu.SemaphoreType.DMA((8,)),
            pltpu.SemaphoreType.DMA((12,)),
        ],
        compiler_params=pltpu.CompilerParams(
            collective_id=0, has_side_effects=True, vmem_limit_bytes=60 * 1024 * 1024
        ),
    )(*operands)
    return result.reshape(bins, width_x, width_y)


def solution(mesh):
    return jax.shard_map(
        functools.partial(body, mesh.shape["gx"], mesh.shape["gy"]),
        mesh=mesh,
        in_specs=(
            P(None, "gx", "gy"),
            P(None, "gx", "gy"),
            P("gx", "gy"),
            P("gx", "gy"),
            P("gx", "gy"),
            P("gx", "gy"),
            P("gx", "gy"),
            P(),
            P(),
        ),
        out_specs=P(None, "gx", "gy"),
        check_vma=False,
    )
```

```python
import functools

import jax
import jax.numpy as jnp
import numpy as np
from jax import lax
from jax.experimental import pallas as pl
from jax.experimental.pallas import tpu as pltpu
from jax.sharding import PartitionSpec as P

SUBSTEPS = 4
PART = 16
BEFORE = 8
AFTER = 6
LEAD = 0
BESIDE = 4
F32 = jnp.float32
BF16 = jnp.bfloat16


def dft_tables(bins):
    order = np.arange(bins)
    order = np.concatenate([order[:PART // 2], order[-(PART // 2):], order[PART // 2:-(PART // 2)]])
    freq = 2 * order + 1
    index = np.arange(bins)

    def chunked(real, imag):
        pieces = [t[c:c + PART] for c in range(0, bins, PART) for t in (real, imag)]
        return np.concatenate(pieces, axis=0)

    angle = np.pi * (freq[:, None] * index[None, :] % (4 * bins)) / (2 * bins)
    forward = chunked(np.cos(angle), -np.sin(angle))

    def inverse(outputs):
        phase = np.pi * (freq[:, None] * outputs[None, :] % (4 * bins)) / (2 * bins)
        return chunked(np.cos(phase), -np.sin(phase)).T / bins

    gain = inverse(index - 1) * (index > 0)[:, None]
    lag = inverse(index + 1) - inverse(0 * index)
    return tuple(np.asarray(t, np.float32) for t in (forward, gain, lag))


def split(values):
    high = values.astype(BF16)
    low = (values - high.astype(F32)).astype(BF16)
    return high, low


def dot(table, values):
    return jnp.dot(table, values, preferred_element_type=F32)


def rows(*values):
    return jnp.concatenate(values, axis=0)


def product(ar, ai, br, bi):
    return rows(ar * br - ai * bi, ar * bi + ai * br)


def product_conj(lr, li, vr, vi):
    return rows(lr * vr + li * vi, li * vr - lr * vi)


def quarters(chunk):
    return tuple(chunk[q * PART:(q + 1) * PART] for q in range(chunk.shape[0] // PART))


def first_precise(chunks):
    return [chunks[0], *(c.astype(BF16) for c in chunks[1:])]


def high_low(chunks):
    high, low = split(chunks[0])
    return [high, *chunks[1:]], low


def kernel(
    n_gx, n_gy, width_x,
    *refs,
):
    inputs, refs = refs[:12], refs[12:]
    out, refs = refs[0], refs[1:]
    fetched, refs = refs[:12], refs[12:]
    conc, adj, sx, sy, cx, cy, active, ka_ref, kb_ref, fwd_ref, gain_ref, lag_ref = fetched
    (wide, wide_adj, state, lam, y_send, y_recv, z_send, z_recv, own, faces, near, t_fwd, t_gain, t_lam, t_lag, weights,
     send_sem, recv_sem, in_sem) = refs
    fetches = [pltpu.make_async_copy(i, f, in_sem.at[k]) for k, (i, f) in enumerate(zip(inputs, fetched))]
    for k in (0, 2, 3, 4, 5, 1, 7, 8, 9, 10, 11, 6):
        fetches[k].start()
    bins = ka_ref.shape[1]
    width_y = sx.shape[1]
    gx = lax.axis_index("gx")
    gy = lax.axis_index("gy")
    nxt_x, prv_x = lax.rem(gx + 1, n_gx), lax.rem(gx + n_gx - 1, n_gx)
    nxt_y, prv_y = jnp.minimum(gy + 1, n_gy - 1), jnp.maximum(gy - 1, 0)
    has_prv, has_nxt = gy > 0, gy < n_gy - 1
    mesh_id = pl.DeviceIdType.MESH

    barrier = pltpu.get_barrier_semaphore()
    pl.semaphore_signal(barrier, inc=1, device_id=(prv_x, gy), device_id_type=mesh_id)
    pl.semaphore_signal(barrier, inc=1, device_id=(nxt_x, gy), device_id_type=mesh_id)

    @pl.when(has_prv)
    def _():
        pl.semaphore_signal(barrier, inc=1, device_id=(gx, prv_y), device_id_type=mesh_id)

    @pl.when(has_nxt)
    def _():
        pl.semaphore_signal(barrier, inc=1, device_id=(gx, nxt_y), device_id_type=mesh_id)

    span = width_y // width_x
    lane = lax.broadcasted_iota(jnp.int32, (bins, width_y), 1)
    owner, place = lane // span, lane % span
    lane_x = lax.broadcasted_iota(jnp.int32, (width_x, width_y), 1)
    owner_x = lane_x // span

    def shift_of(x):
        return (width_x - 1 - x) * span + span // 2

    def pack_steps(slab_of, owners, results):
        packed = pltpu.roll(slab_of(width_x - 1), span // 2, 1)
        for x in range(width_x - 1):
            packed = jnp.where(owners == width_x - 1 - x, pltpu.roll(slab_of(x), shift_of(x), 1), packed)
            if x % 2:
                yield
        results.append(packed)

    def pack(slab_of, owners):
        results = []
        run(pack_steps(slab_of, owners, results))
        return results[0]

    def unpack(packed, x):
        return pltpu.roll(packed, width_y - shift_of(x), 1)

    def run(steps, count=None):
        if count is None:
            for _ in steps:
                pass
        else:
            for _ in range(count):
                next(steps, None)

    def weave(steps, others, count):
        total = 2 * SUBSTEPS
        for index in range(total):
            run(others, (index + 1) * count // total - index * count // total)
            run(steps, 1)
        run(steps)

    pieces = span // 2
    depth = bins // pieces
    shelf = ((place[:depth] + span - (pieces - 1)) % span) // 2

    def thin(packed):
        result = packed[:depth]
        for piece in range(1, pieces):
            part = pltpu.roll(packed[piece * depth:(piece + 1) * depth], 2 * piece, 1)
            result = jnp.where(shelf == piece, part, result)
        return result

    def widen(thinned):
        return rows(thinned, *(pltpu.roll(thinned, width_y - 2 * piece, 1) for piece in range(1, pieces)))

    for k in (2, 3, 4, 5):
        fetches[k].wait()
    plus_x = sx[...].astype(F32)
    plus_y = sy[...].astype(F32)
    inside = (lane_x + gy * width_y > 0).astype(F32)
    ux = cx[...] * plus_x
    bx = cx[...] * (1.0 - plus_x)
    uy = cy[...] * plus_y * inside
    by = cy[...] * (1.0 - plus_y) * inside

    ux_next, bx_next = (rows(v[1:], v[:1]) for v in (ux, bx))
    uy_next, by_next = (pltpu.roll(v, width_y - 1, 1) for v in (uy, by))
    centre = 1.0 - bx - ux_next - by - uy_next
    faces[...] = jnp.zeros(faces.shape, F32)
    for index, values in enumerate((uy, by, ux, bx, ux_next, bx_next, uy_next, by_next, centre)):
        faces[pl.ds(index, width_x, stride=16), :] = values

    fetches[0].wait()
    wide[...] = conc[...].astype(F32)
    for x in (0, width_x - 1):
        state[x + 1, :bins, :] = wide[pl.ds(x, bins, stride=width_x), :]
    state[1, bins:bins + 1, :] = ux[0:1]
    state[1, bins + 1:bins + 2, :] = bx[0:1]
    state[1, bins + 2:, :] = jnp.zeros((6, width_y), F32)
    state[width_x, bins:, :] = jnp.zeros((8, width_y), F32)

    def x_copies(field, base):
        return (
            pltpu.make_async_remote_copy(
                src_ref=field.at[1], dst_ref=field.at[width_x + 1],
                send_sem=send_sem.at[base], recv_sem=recv_sem.at[base],
                device_id=(prv_x, gy), device_id_type=mesh_id),
            pltpu.make_async_remote_copy(
                src_ref=field.at[width_x], dst_ref=field.at[0],
                send_sem=send_sem.at[base + 1], recv_sem=recv_sem.at[base + 1],
                device_id=(nxt_x, gy), device_id_type=mesh_id),
        )

    pl.semaphore_wait(barrier, 2 + has_prv.astype(jnp.int32) + has_nxt.astype(jnp.int32))
    first_x = x_copies(state, 0)
    for copy in first_x:
        copy.start()
    for x in range(1, width_x - 1):
        state[x + 1, :bins, :] = wide[pl.ds(x, bins, stride=width_x), :]

    packed = pack(lambda x: state[x + 1, :bins, :].astype(BF16), owner).astype(F32)
    own[...] = packed
    y_send[:depth, :] = thin(packed)
    y_send[depth:, :] = pack(lambda x: faces[x * 16:x * 16 + 8, :], owner[:8])

    def y_copies(source, target, base):
        return (
            pltpu.make_async_remote_copy(
                src_ref=source, dst_ref=target.at[1],
                send_sem=send_sem.at[base], recv_sem=recv_sem.at[base],
                device_id=(gx, prv_y), device_id_type=mesh_id),
            pltpu.make_async_remote_copy(
                src_ref=source, dst_ref=target.at[0],
                send_sem=send_sem.at[base + 1], recv_sem=recv_sem.at[base + 1],
                device_id=(gx, nxt_y), device_id_type=mesh_id),
        )

    def start_y(copies, target):
        to_prv, to_nxt = copies

        @pl.when(has_prv)
        def _():
            to_prv.start()

        @pl.when(has_nxt)
        def _():
            to_nxt.start()

        @pl.when(jnp.logical_not(has_prv))
        def _():
            target[0] = jnp.zeros(target.shape[1:], F32)

        @pl.when(jnp.logical_not(has_nxt))
        def _():
            target[1] = jnp.zeros(target.shape[1:], F32)

    def wait_y(copies):
        to_prv, to_nxt = copies

        @pl.when(has_prv)
        def _():
            to_prv.wait_send()
            to_nxt.wait_recv()

        @pl.when(has_nxt)
        def _():
            to_nxt.wait_send()
            to_prv.wait_recv()

    first_y = y_copies(y_send, y_recv, 2)
    start_y(first_y, y_recv)

    for k in (7, 8, 9, 10, 11):
        fetches[k].wait()
    ka_row, kb_row = ka_ref[...], kb_ref[...]
    weights[0] = jnp.broadcast_to(ka_row, (bins, bins)).T
    weights[1] = jnp.broadcast_to(kb_row, (bins, bins)).T
    ka_col, kb_col = weights[0], weights[1]
    first, corrected = 2 * PART, 4 * PART
    forward = fwd_ref[...]
    ah, al = split(forward * ka_row)
    bh, bl = split(forward * kb_row)
    lh, ll = split(forward)
    blank = jnp.zeros((PART, bins), BF16)
    for c in range(bins // PART):
        for q, high in enumerate((ah, bh)):
            there = slice(c * corrected + q * first, c * corrected + (q + 1) * first)
            t_fwd[there, :bins] = high[c * first:(c + 1) * first]
            t_fwd[there, bins:] = high[c * first:(c + 1) * first]
    sums, rest = 4 * bins, 4 * bins + PART
    empty = jnp.zeros((PART - 4, bins), F32)
    high, low = ((v.astype(F32)) for v in split(rows(ka_row, kb_row)))
    t_fwd[sums:rest, :bins] = rows(high, low, empty).astype(BF16)
    t_fwd[sums:rest, bins:] = rows(high, 0.0 * low, empty).astype(BF16)
    t_fwd[rest:, :bins] = rows(al[:first], bl[:first])
    t_fwd[rest:, bins:] = rows(*[blank] * 4)
    t_lam[:2 * bins, :bins] = lh
    t_lam[:2 * bins, bins:] = lh
    t_lam[2 * bins:, :bins] = ll[:first]
    t_lam[2 * bins:, bins:] = rows(blank, blank)
    high, low = split(gain_ref[...])
    t_gain[:, :2 * bins] = high
    t_gain[:, 2 * bins:2 * bins + first] = high[:, :first]
    t_gain[:, 2 * bins + first:] = low[:, :first]
    lag = lag_ref[...]
    ka_col2 = jnp.concatenate([ka_col, ka_col], axis=1)
    kb_col2 = jnp.concatenate([kb_col, kb_col], axis=1)
    ah, al = split(ka_col2 * lag)
    bh, bl = split(kb_col2 * lag)
    t_lag[:, :2 * bins] = ah
    t_lag[:, 2 * bins:4 * bins] = bh
    t_lag[:, 4 * bins:] = jnp.concatenate([ah[:, :first], bh[:, :first], al[:, :first], bl[:, :first]], axis=1)

    fetches[1].wait()
    fetches[6].wait()
    wide_adj[...] = adj[...].astype(F32)
    ending = lambda x: wide_adj[pl.ds(x, bins, stride=width_x), :]

    def stencil(field, x, low_x, high_x, low_y, high_y):
        slab = field[x + 1, :bins, :]
        row = lambda k: faces[x * 16 + k:x * 16 + k + 1, :]
        return (
            slab * row(8)
            + row(low_x) * field[x, :bins, :]
            + row(high_x) * field[x + 2, :bins, :]
            + row(low_y) * pltpu.roll(slab, 1, 1)
            + row(high_y) * pltpu.roll(slab, width_y - 1, 1)
        )

    def packed_stencil(packed, rows_x, rows_y, low_x, high_x, low_y, high_y):
        row = lambda k: near[k:k + 1, :]
        x_before, x_after = rows_x
        x_before = jnp.where(
            owner == width_x - 1, pltpu.roll(x_before, width_y - span // 2, 1), pltpu.roll(packed, width_y - span, 1))
        x_after = jnp.where(owner == 0, pltpu.roll(x_after, span // 2, 1), pltpu.roll(packed, span, 1))
        y_before = pltpu.roll(jnp.where(place == span // 2 - 1, rows_y[0], packed), 1, 1)
        y_after = pltpu.roll(jnp.where(place == span // 2, rows_y[1], packed), width_y - 1, 1)
        return (packed * row(8) + row(low_x) * x_before + row(high_x) * x_after
                + row(low_y) * y_before + row(high_y) * y_after)

    def beside(values):
        return jnp.concatenate(list(values), axis=1)

    def forward_steps(block, saved):
        current = beside(cell[0] for cell in block)
        ka = beside(weights[0] for _ in block)
        kb = beside(weights[1] for _ in block)
        for step in range(SUBSTEPS):
            high, low = split(current)
            result = dot(t_fwd[...], rows(high, low))
            yield
            spectra = [result[c:c + corrected] for c in range(0, sums, corrected)]
            spectra[0] = spectra[0] + result[rest:rest + corrected]
            spectra = [quarters(chunk) for chunk in first_precise(spectra)]
            total_a, total_b = (
                result[sums + k:sums + k + 1] + result[sums + 2 + k:sums + 3 + k] for k in (0, 1))
            loss = ka * total_b + kb * total_a
            saved.append((spectra, loss))
            if step < SUBSTEPS - 1:
                high, low = high_low([product(*chunk) for chunk in spectra])
                current = current + dot(t_gain[...], rows(*high, low, high[0])) - current * loss
            yield

    def backward_steps(block, saved, results):
        start = beside(cell[1] for cell in block)
        adjoint = start
        for spectra, loss in reversed(saved):
            high, low = split(adjoint)
            result = dot(t_lam[...], rows(high, low))
            yield
            spectra_l = [result[c:c + first] for c in range(0, 2 * bins, first)]
            spectra_l[0] = spectra_l[0] + result[2 * bins:]
            spectra_l = [quarters(chunk) for chunk in first_precise(spectra_l)]
            high_b, low_b = high_low([product_conj(*l, *v[2:]) for l, v in zip(spectra_l, spectra)])
            high_a, low_a = high_low([product_conj(*l, *v[:2]) for l, v in zip(spectra_l, spectra)])
            terms = rows(*high_b, *high_a, low_b, low_a, high_b[0], high_a[0])
            adjoint = adjoint + dot(t_lag[...], terms) - adjoint * loss
            yield
        on = beside(cell[2] for cell in block) == 1
        result = jnp.where(on, adjoint, start)
        results += [result[:, index * width_y:(index + 1) * width_y] for index in range(len(block))]

    def cells_of(x):
        return stencil(state, x, 2, 5, 0, 7), ending(x), active[pl.ds(x, 1), :]

    class Group:
        def __init__(self, places, cells):
            self.places, self.cells = places, cells
            self.saved, self.results = [], []

        def forward(self):
            return forward_steps(self.cells, self.saved)

        def backward(self):
            return backward_steps(self.cells, self.saved, self.results)

        def put(self):
            for x, result in zip(self.places, self.results):
                lam[x + 1] = result

    inner = iter(range(1, width_x - 1))
    take = lambda count: [next(inner) for _ in range(count)]
    ends = (0, width_x - 1)
    places = take(BEFORE)
    early = Group(places, [cells_of(x) for x in places])
    middle_places = [*ends, *take(width_x - 2 - BEFORE - AFTER)]
    late = Group(take(AFTER), [])
    packed_ending, near_faces = [], []
    last = 16 * (width_x - 1)

    def prepare():
        yield from pack_steps(lambda x: faces[x * 16:(x + 1) * 16, :], owner[:16], near_faces)
        near[...] = near_faces[0]
        yield from pack_steps(ending, owner, packed_ending)
        for x in late.places:
            late.cells.append(cells_of(x))
            yield

    preparing = prepare()
    weave(early.forward(), preparing, width_x + AFTER)
    run(preparing)
    packed_active = pack(lambda x: active[pl.ds(x, 1), :], owner[:1])
    early_steps = early.backward()
    run(early_steps, LEAD)

    wait_y(first_y)
    for copy in first_x:
        copy.wait()
    y_faces = pltpu.roll(y_recv[1, depth:, :], width_y - 1, 1)
    x_faces = pltpu.roll(state[width_x + 1, bins:, :], span // 2, 1)
    edge_faces = near_faces[0]
    for k in (0, 1):
        near[4 + k:5 + k, :] = jnp.where(owner[:1] == 0, x_faces[k:k + 1], edge_faces[4 + k:5 + k])
        near[6 + k:7 + k, :] = jnp.where(place[:1] == span // 2 - 1, y_faces[k:k + 1], edge_faces[6 + k:7 + k])
        faces[last + 4 + k:last + 5 + k, :] = state[width_x + 1, bins + k:bins + k + 1, :]
    near[8:9, :] = 1.0 - near[3:4, :] - near[4:5, :] - near[1:2, :] - near[6:7, :]
    faces[last + 8:last + 9, :] = (1.0 - faces[last + 3:last + 4, :] - faces[last + 4:last + 5, :]
                                   - faces[last + 1:last + 2, :] - faces[last + 6:last + 7, :])
    packed = packed_stencil(
        own[...], (state[0, :bins, :], state[width_x + 1, :bins, :]),
        (widen(y_recv[0, :depth, :]), widen(y_recv[1, :depth, :])), 2, 5, 0, 7)
    edges = Group(
        middle_places, [(packed, packed_ending[0], packed_active)] + [cells_of(x) for x in middle_places])
    weave(edges.forward(), early_steps, 2 * SUBSTEPS - LEAD)
    run(early_steps)
    early.put()
    late_steps = late.forward()
    weave(edges.backward(), late_steps, BESIDE)
    packed, *edges.results = edges.results
    own[...] = packed
    z_send[...] = thin(packed)
    edge = (lane == 0) | (lane == width_y - 1)
    for k, x in enumerate(ends):
        edges.results[k] = jnp.where(edge, unpack(packed, x), edges.results[k])
    edges.put()
    second_y = y_copies(z_send, z_recv, 6)
    start_y(second_y, z_recv)
    second_x = x_copies(lam, 4)
    for copy in second_x:
        copy.start()

    def finish(places):
        for x in places:
            out[pl.ds(x, bins, stride=width_x), :] = stencil(lam, x, 3, 4, 1, 6)
            yield

    run(late_steps)
    weave(late.backward(), finish(range(1, BEFORE)), BEFORE - 1)
    late.put()
    run(finish(range(BEFORE, width_x - 1)))

    wait_y(second_y)
    for copy in second_x:
        copy.wait()
    run(finish(ends))
    packed = packed_stencil(
        own[...], (lam[0], lam[width_x + 1]), (widen(z_recv[0]), widen(z_recv[1])), 3, 4, 1, 6)
    own[...] = packed
    near_edge = ((lane < 2) | (lane >= width_y - 2))[:8]
    for b in range(bins):
        for x in range(0, width_x, 8):
            here = slice(b * width_x + x, b * width_x + x + 8)
            cells = jnp.broadcast_to(own[b:b + 1, :], (8, width_y))
            cells = pltpu.roll(cells, width_y - shift_of(x), 1, stride=span, stride_axis=0)
            out[here, :] = jnp.where(near_edge, cells, out[here, :])


def body(n_gx, n_gy, concentration, adjoint_next, sign_x, sign_y, courant_x, courant_y, active, kernel_a, kernel_b):
    bins, width_x, width_y = concentration.shape
    cells = bins * width_x
    depth = bins * 2 * width_x // width_y
    tables = dft_tables(bins)
    operands = (
        concentration.reshape(cells, width_y),
        adjoint_next.reshape(cells, width_y),
        sign_x, sign_y, courant_x, courant_y, active,
        kernel_a.reshape(1, bins), kernel_b.reshape(1, bins),
        *(jnp.asarray(t) for t in tables),
    )
    result = pl.pallas_call(
        functools.partial(kernel, n_gx, n_gy, width_x),
        out_shape=pltpu.VMEM((cells, width_y), F32),
        in_specs=[pl.BlockSpec(memory_space=pltpu.HBM)] * 12,
        out_specs=pl.BlockSpec(memory_space=pltpu.VMEM),
        scratch_shapes=[
            *(pltpu.VMEM(a.shape, a.dtype) for a in operands),
            pltpu.VMEM((cells, width_y), F32),
            pltpu.VMEM((cells, width_y), F32),
            pltpu.VMEM((width_x + 2, bins + 8, width_y), F32),
            pltpu.VMEM((width_x + 2, bins, width_y), F32),
            pltpu.VMEM((depth + 8, width_y), F32),
            pltpu.VMEM((2, depth + 8, width_y), F32),
            pltpu.VMEM((depth, width_y), F32),
            pltpu.VMEM((2, depth, width_y), F32),
            pltpu.VMEM((bins, width_y), F32),
            pltpu.VMEM((16 * width_x, width_y), F32),
            pltpu.VMEM((16, width_y), F32),
            pltpu.VMEM((4 * bins + 5 * PART, 2 * bins), BF16),
            pltpu.VMEM((bins, 2 * bins + 4 * PART), BF16),
            pltpu.VMEM((2 * bins + 2 * PART, 2 * bins), BF16),
            pltpu.VMEM((bins, 4 * bins + 8 * PART), BF16),
            pltpu.VMEM((2, bins, bins), F32),
            pltpu.SemaphoreType.DMA((8,)),
            pltpu.SemaphoreType.DMA((8,)),
            pltpu.SemaphoreType.DMA((12,)),
        ],
        compiler_params=pltpu.CompilerParams(
            collective_id=0, has_side_effects=True, vmem_limit_bytes=60 * 1024 * 1024
        ),
    )(*operands)
    return result.reshape(bins, width_x, width_y)


def solution(mesh):
    return jax.shard_map(
        functools.partial(body, mesh.shape["gx"], mesh.shape["gy"]),
        mesh=mesh,
        in_specs=(
            P(None, "gx", "gy"),
            P(None, "gx", "gy"),
            P("gx", "gy"),
            P("gx", "gy"),
            P("gx", "gy"),
            P("gx", "gy"),
            P("gx", "gy"),
            P(),
            P(),
        ),
        out_specs=P(None, "gx", "gy"),
        check_vma=False,
    )
```

```python
import functools

import jax
import jax.numpy as jnp
import numpy as np
from jax import lax
from jax.experimental import pallas as pl
from jax.experimental.pallas import tpu as pltpu
from jax.sharding import PartitionSpec as P

SUBSTEPS = 4
PART = 16
BEFORE = 8
AFTER = 6
LEAD = 0
BESIDE = 4
F32 = jnp.float32
BF16 = jnp.bfloat16


def dft_tables(bins):
    order = np.arange(bins)
    order = np.concatenate([order[:PART // 2], order[-(PART // 2):], order[PART // 2:-(PART // 2)]])
    freq = 2 * order + 1
    index = np.arange(bins)

    def chunked(real, imag):
        pieces = [t[c:c + PART] for c in range(0, bins, PART) for t in (real, imag)]
        return np.concatenate(pieces, axis=0)

    angle = np.pi * (freq[:, None] * index[None, :] % (4 * bins)) / (2 * bins)
    forward = chunked(np.cos(angle), -np.sin(angle))

    def inverse(outputs):
        phase = np.pi * (freq[:, None] * outputs[None, :] % (4 * bins)) / (2 * bins)
        return chunked(np.cos(phase), -np.sin(phase)).T / bins

    gain = inverse(index - 1) * (index > 0)[:, None]
    lag = inverse(index + 1) - inverse(0 * index)
    return tuple(np.asarray(t, np.float32) for t in (forward, gain, lag))


def split(values):
    high = values.astype(BF16)
    low = (values - high.astype(F32)).astype(BF16)
    return high, low


def dot(table, values):
    return jnp.dot(table, values, preferred_element_type=F32)


def rows(*values):
    return jnp.concatenate(values, axis=0)


def product(ar, ai, br, bi):
    return rows(ar * br - ai * bi, ar * bi + ai * br)


def product_conj(lr, li, vr, vi):
    return rows(lr * vr + li * vi, li * vr - lr * vi)


def quarters(chunk):
    return tuple(chunk[q * PART:(q + 1) * PART] for q in range(chunk.shape[0] // PART))


def first_precise(chunks):
    return [chunks[0], *(c.astype(BF16) for c in chunks[1:])]


def high_low(chunks):
    high, low = split(chunks[0])
    return [high, *chunks[1:]], low


def kernel(
    n_gx, n_gy, width_x,
    *refs,
):
    inputs, refs = refs[:12], refs[12:]
    out, refs = refs[0], refs[1:]
    fetched, refs = refs[:12], refs[12:]
    conc, adj, sx, sy, cx, cy, active, ka_ref, kb_ref, fwd_ref, gain_ref, lag_ref = fetched
    (wide, wide_adj, state, lam, y_send, y_recv, z_send, z_recv, own, faces, near, t_fwd, t_gain, t_lam, t_lag, weights,
     send_sem, recv_sem, in_sem) = refs
    fetches = [pltpu.make_async_copy(i, f, in_sem.at[k]) for k, (i, f) in enumerate(zip(inputs, fetched))]
    for k in (0, 2, 3, 4, 5, 1, 7, 8, 9, 10, 11, 6):
        fetches[k].start()
    bins = ka_ref.shape[1]
    width_y = sx.shape[1]
    gx = lax.axis_index("gx")
    gy = lax.axis_index("gy")
    nxt_x, prv_x = lax.rem(gx + 1, n_gx), lax.rem(gx + n_gx - 1, n_gx)
    nxt_y, prv_y = jnp.minimum(gy + 1, n_gy - 1), jnp.maximum(gy - 1, 0)
    has_prv, has_nxt = gy > 0, gy < n_gy - 1
    mesh_id = pl.DeviceIdType.MESH

    barrier = pltpu.get_barrier_semaphore()
    pl.semaphore_signal(barrier, inc=1, device_id=(prv_x, gy), device_id_type=mesh_id)
    pl.semaphore_signal(barrier, inc=1, device_id=(nxt_x, gy), device_id_type=mesh_id)

    @pl.when(has_prv)
    def _():
        pl.semaphore_signal(barrier, inc=1, device_id=(gx, prv_y), device_id_type=mesh_id)

    @pl.when(has_nxt)
    def _():
        pl.semaphore_signal(barrier, inc=1, device_id=(gx, nxt_y), device_id_type=mesh_id)

    span = width_y // width_x
    lane = lax.broadcasted_iota(jnp.int32, (bins, width_y), 1)
    owner, place = lane // span, lane % span
    lane_x = lax.broadcasted_iota(jnp.int32, (width_x, width_y), 1)
    owner_x = lane_x // span

    def shift_of(x):
        return (width_x - 1 - x) * span + span // 2

    def pack_steps(slab_of, owners, results):
        packed = pltpu.roll(slab_of(width_x - 1), span // 2, 1)
        for x in range(width_x - 1):
            packed = jnp.where(owners == width_x - 1 - x, pltpu.roll(slab_of(x), shift_of(x), 1), packed)
            if x % 2:
                yield
        results.append(packed)

    def pack(slab_of, owners):
        results = []
        run(pack_steps(slab_of, owners, results))
        return results[0]

    def unpack(packed, x):
        return pltpu.roll(packed, width_y - shift_of(x), 1)

    def run(steps, count=None):
        if count is None:
            for _ in steps:
                pass
        else:
            for _ in range(count):
                next(steps, None)

    def weave(steps, others, count):
        total = 2 * SUBSTEPS
        for index in range(total):
            run(others, (index + 1) * count // total - index * count // total)
            run(steps, 1)
        run(steps)

    pieces = span // 2
    depth = bins // pieces
    shelf = ((place[:depth] + span - (pieces - 1)) % span) // 2

    def thin(packed):
        result = packed[:depth]
        for piece in range(1, pieces):
            part = pltpu.roll(packed[piece * depth:(piece + 1) * depth], 2 * piece, 1)
            result = jnp.where(shelf == piece, part, result)
        return result

    def widen(thinned):
        return rows(thinned, *(pltpu.roll(thinned, width_y - 2 * piece, 1) for piece in range(1, pieces)))

    for k in (2, 3, 4, 5):
        fetches[k].wait()
    plus_x = sx[...].astype(F32)
    plus_y = sy[...].astype(F32)
    inside = (lane_x + gy * width_y > 0).astype(F32)
    ux = cx[...] * plus_x
    bx = cx[...] * (1.0 - plus_x)
    uy = cy[...] * plus_y * inside
    by = cy[...] * (1.0 - plus_y) * inside

    ux_next, bx_next = (rows(v[1:], v[:1]) for v in (ux, bx))
    uy_next, by_next = (pltpu.roll(v, width_y - 1, 1) for v in (uy, by))
    centre = 1.0 - bx - ux_next - by - uy_next
    faces[...] = jnp.zeros(faces.shape, F32)
    for index, values in enumerate((uy, by, ux, bx, ux_next, bx_next, uy_next, by_next, centre)):
        faces[pl.ds(index, width_x, stride=16), :] = values

    fetches[0].wait()
    wide[...] = conc[...].astype(F32)
    for x in (0, width_x - 1):
        state[x + 1, :bins, :] = wide[pl.ds(x, bins, stride=width_x), :]
    state[1, bins:bins + 1, :] = ux[0:1]
    state[1, bins + 1:bins + 2, :] = bx[0:1]
    state[1, bins + 2:, :] = jnp.zeros((6, width_y), F32)
    state[width_x, bins:, :] = jnp.zeros((8, width_y), F32)

    def x_copies(field, base):
        return (
            pltpu.make_async_remote_copy(
                src_ref=field.at[1], dst_ref=field.at[width_x + 1],
                send_sem=send_sem.at[base], recv_sem=recv_sem.at[base],
                device_id=(prv_x, gy), device_id_type=mesh_id),
            pltpu.make_async_remote_copy(
                src_ref=field.at[width_x], dst_ref=field.at[0],
                send_sem=send_sem.at[base + 1], recv_sem=recv_sem.at[base + 1],
                device_id=(nxt_x, gy), device_id_type=mesh_id),
        )

    pl.semaphore_wait(barrier, 2 + has_prv.astype(jnp.int32) + has_nxt.astype(jnp.int32))
    first_x = x_copies(state, 0)
    for copy in first_x:
        copy.start()
    for x in range(1, width_x - 1):
        state[x + 1, :bins, :] = wide[pl.ds(x, bins, stride=width_x), :]

    packed = pack(lambda x: state[x + 1, :bins, :].astype(BF16), owner).astype(F32)
    own[...] = packed
    y_send[:depth, :] = thin(packed)
    y_send[depth:, :] = pack(lambda x: faces[x * 16:x * 16 + 8, :], owner[:8])

    def y_copies(source, target, base):
        return (
            pltpu.make_async_remote_copy(
                src_ref=source, dst_ref=target.at[1],
                send_sem=send_sem.at[base], recv_sem=recv_sem.at[base],
                device_id=(gx, prv_y), device_id_type=mesh_id),
            pltpu.make_async_remote_copy(
                src_ref=source, dst_ref=target.at[0],
                send_sem=send_sem.at[base + 1], recv_sem=recv_sem.at[base + 1],
                device_id=(gx, nxt_y), device_id_type=mesh_id),
        )

    def start_y(copies, target):
        to_prv, to_nxt = copies

        @pl.when(has_prv)
        def _():
            to_prv.start()

        @pl.when(has_nxt)
        def _():
            to_nxt.start()

        @pl.when(jnp.logical_not(has_prv))
        def _():
            target[0] = jnp.zeros(target.shape[1:], F32)

        @pl.when(jnp.logical_not(has_nxt))
        def _():
            target[1] = jnp.zeros(target.shape[1:], F32)

    def wait_y(copies):
        to_prv, to_nxt = copies

        @pl.when(has_prv)
        def _():
            to_prv.wait_send()
            to_nxt.wait_recv()

        @pl.when(has_nxt)
        def _():
            to_nxt.wait_send()
            to_prv.wait_recv()

    first_y = y_copies(y_send, y_recv, 2)
    start_y(first_y, y_recv)

    for k in (7, 8, 9, 10, 11):
        fetches[k].wait()
    ka_row, kb_row = ka_ref[...], kb_ref[...]
    weights[0] = jnp.broadcast_to(ka_row, (bins, bins)).T
    weights[1] = jnp.broadcast_to(kb_row, (bins, bins)).T
    ka_col, kb_col = weights[0], weights[1]
    first, corrected = 2 * PART, 4 * PART
    forward = fwd_ref[...]
    ah, al = split(forward * ka_row)
    bh, bl = split(forward * kb_row)
    lh, ll = split(forward)
    blank = jnp.zeros((PART, bins), BF16)
    for c in range(bins // PART):
        for q, high in enumerate((ah, bh)):
            there = slice(c * corrected + q * first, c * corrected + (q + 1) * first)
            t_fwd[there, :bins] = high[c * first:(c + 1) * first]
            t_fwd[there, bins:] = high[c * first:(c + 1) * first]
    sums, rest = 4 * bins, 4 * bins + PART
    empty = jnp.zeros((PART - 4, bins), F32)
    high, low = ((v.astype(F32)) for v in split(rows(ka_row, kb_row)))
    t_fwd[sums:rest, :bins] = rows(high, low, empty).astype(BF16)
    t_fwd[sums:rest, bins:] = rows(high, 0.0 * low, empty).astype(BF16)
    t_fwd[rest:, :bins] = rows(al[:first], bl[:first])
    t_fwd[rest:, bins:] = rows(*[blank] * 4)
    t_lam[:2 * bins, :bins] = lh
    t_lam[:2 * bins, bins:] = lh
    t_lam[2 * bins:, :bins] = ll[:first]
    t_lam[2 * bins:, bins:] = rows(blank, blank)
    high, low = split(gain_ref[...])
    t_gain[:, :2 * bins] = high
    t_gain[:, 2 * bins:2 * bins + first] = high[:, :first]
    t_gain[:, 2 * bins + first:] = low[:, :first]
    lag = lag_ref[...]
    ka_col2 = jnp.concatenate([ka_col, ka_col], axis=1)
    kb_col2 = jnp.concatenate([kb_col, kb_col], axis=1)
    ah, al = split(ka_col2 * lag)
    bh, bl = split(kb_col2 * lag)
    t_lag[:, :2 * bins] = ah
    t_lag[:, 2 * bins:4 * bins] = bh
    t_lag[:, 4 * bins:] = jnp.concatenate([ah[:, :first], bh[:, :first], al[:, :first], bl[:, :first]], axis=1)

    fetches[1].wait()
    fetches[6].wait()
    wide_adj[...] = adj[...].astype(F32)
    ending = lambda x: wide_adj[pl.ds(x, bins, stride=width_x), :]

    def stencil(field, x, low_x, high_x, low_y, high_y):
        slab = field[x + 1, :bins, :]
        row = lambda k: faces[x * 16 + k:x * 16 + k + 1, :]
        return (
            slab * row(8)
            + row(low_x) * field[x, :bins, :]
            + row(high_x) * field[x + 2, :bins, :]
            + row(low_y) * pltpu.roll(slab, 1, 1)
            + row(high_y) * pltpu.roll(slab, width_y - 1, 1)
        )

    def packed_stencil(packed, rows_x, rows_y, low_x, high_x, low_y, high_y):
        row = lambda k: near[k:k + 1, :]
        x_before, x_after = rows_x
        x_before = jnp.where(
            owner == width_x - 1, pltpu.roll(x_before, width_y - span // 2, 1), pltpu.roll(packed, width_y - span, 1))
        x_after = jnp.where(owner == 0, pltpu.roll(x_after, span // 2, 1), pltpu.roll(packed, span, 1))
        y_before = pltpu.roll(jnp.where(place == span // 2 - 1, rows_y[0], packed), 1, 1)
        y_after = pltpu.roll(jnp.where(place == span // 2, rows_y[1], packed), width_y - 1, 1)
        return (packed * row(8) + row(low_x) * x_before + row(high_x) * x_after
                + row(low_y) * y_before + row(high_y) * y_after)

    def beside(values):
        return jnp.concatenate(list(values), axis=1)

    def forward_steps(block, saved):
        current = beside(cell[0] for cell in block)
        ka = beside(weights[0] for _ in block)
        kb = beside(weights[1] for _ in block)
        for step in range(SUBSTEPS):
            high, low = split(current)
            result = dot(t_fwd[...], rows(high, low))
            yield
            spectra = [result[c:c + corrected] for c in range(0, sums, corrected)]
            spectra[0] = spectra[0] + result[rest:rest + corrected]
            spectra = [quarters(chunk) for chunk in first_precise(spectra)]
            total_a, total_b = (
                result[sums + k:sums + k + 1] + result[sums + 2 + k:sums + 3 + k] for k in (0, 1))
            loss = ka * total_b + kb * total_a
            saved.append((spectra, loss))
            if step < SUBSTEPS - 1:
                high, low = high_low([product(*chunk) for chunk in spectra])
                current = current + dot(t_gain[...], rows(*high, low, high[0])) - current * loss
            yield

    def backward_steps(block, saved, results):
        start = beside(cell[1] for cell in block)
        adjoint = start
        for spectra, loss in reversed(saved):
            high, low = split(adjoint)
            result = dot(t_lam[...], rows(high, low))
            yield
            spectra_l = [result[c:c + first] for c in range(0, 2 * bins, first)]
            spectra_l[0] = spectra_l[0] + result[2 * bins:]
            spectra_l = [quarters(chunk) for chunk in first_precise(spectra_l)]
            high_b, low_b = high_low([product_conj(*l, *v[2:]) for l, v in zip(spectra_l, spectra)])
            high_a, low_a = high_low([product_conj(*l, *v[:2]) for l, v in zip(spectra_l, spectra)])
            terms = rows(*high_b, *high_a, low_b, low_a, high_b[0], high_a[0])
            adjoint = adjoint + dot(t_lag[...], terms) - adjoint * loss
            yield
        on = beside(cell[2] for cell in block) == 1
        result = jnp.where(on, adjoint, start)
        results += [result[:, index * width_y:(index + 1) * width_y] for index in range(len(block))]

    def cells_of(x):
        return stencil(state, x, 2, 5, 0, 7), ending(x), active[pl.ds(x, 1), :]

    class Group:
        def __init__(self, places, cells):
            self.places, self.cells = places, cells
            self.saved, self.results = [], []

        def forward(self):
            return forward_steps(self.cells, self.saved)

        def backward(self):
            return backward_steps(self.cells, self.saved, self.results)

        def put(self):
            for x, result in zip(self.places, self.results):
                lam[x + 1] = result

    inner = iter(range(1, width_x - 1))
    take = lambda count: [next(inner) for _ in range(count)]
    ends = (0, width_x - 1)
    places = take(BEFORE)
    early = Group(places, [cells_of(x) for x in places])
    middle_places = [*ends, *take(width_x - 2 - BEFORE - AFTER)]
    late = Group(take(AFTER), [])
    packed_ending, near_faces = [], []
    last = 16 * (width_x - 1)

    def prepare():
        yield from pack_steps(lambda x: faces[x * 16:(x + 1) * 16, :], owner[:16], near_faces)
        near[...] = near_faces[0]
        yield from pack_steps(ending, owner, packed_ending)
        for x in late.places:
            late.cells.append(cells_of(x))
            yield

    preparing = prepare()
    weave(early.forward(), preparing, width_x + AFTER)
    run(preparing)
    packed_active = pack(lambda x: active[pl.ds(x, 1), :], owner[:1])
    early_steps = early.backward()
    run(early_steps, LEAD)

    wait_y(first_y)
    for copy in first_x:
        copy.wait()
    y_faces = pltpu.roll(y_recv[1, depth:, :], width_y - 1, 1)
    x_faces = pltpu.roll(state[width_x + 1, bins:, :], span // 2, 1)
    edge_faces = near_faces[0]
    for k in (0, 1):
        near[4 + k:5 + k, :] = jnp.where(owner[:1] == 0, x_faces[k:k + 1], edge_faces[4 + k:5 + k])
        near[6 + k:7 + k, :] = jnp.where(place[:1] == span // 2 - 1, y_faces[k:k + 1], edge_faces[6 + k:7 + k])
        faces[last + 4 + k:last + 5 + k, :] = state[width_x + 1, bins + k:bins + k + 1, :]
    near[8:9, :] = 1.0 - near[3:4, :] - near[4:5, :] - near[1:2, :] - near[6:7, :]
    faces[last + 8:last + 9, :] = (1.0 - faces[last + 3:last + 4, :] - faces[last + 4:last + 5, :]
                                   - faces[last + 1:last + 2, :] - faces[last + 6:last + 7, :])
    packed = packed_stencil(
        own[...], (state[0, :bins, :], state[width_x + 1, :bins, :]),
        (widen(y_recv[0, :depth, :]), widen(y_recv[1, :depth, :])), 2, 5, 0, 7)
    edges = Group(
        middle_places, [(packed, packed_ending[0], packed_active)] + [cells_of(x) for x in middle_places])
    weave(edges.forward(), early_steps, 2 * SUBSTEPS - LEAD)
    run(early_steps)
    early.put()
    late_steps = late.forward()
    weave(edges.backward(), late_steps, BESIDE)
    packed, *edges.results = edges.results
    own[...] = packed
    z_send[...] = thin(packed)
    edge = (lane == 0) | (lane == width_y - 1)
    for k, x in enumerate(ends):
        edges.results[k] = jnp.where(edge, unpack(packed, x), edges.results[k])
    edges.put()
    second_y = y_copies(z_send, z_recv, 6)
    start_y(second_y, z_recv)
    second_x = x_copies(lam, 4)
    for copy in second_x:
        copy.start()

    def finish(places):
        for x in places:
            out[pl.ds(x, bins, stride=width_x), :] = stencil(lam, x, 3, 4, 1, 6)
            yield

    finishing = finish(range(1, BEFORE))
    weave(late_steps, finishing, BEFORE - 1)
    run(finishing)
    run(late.backward())
    late.put()
    run(finish(range(BEFORE, width_x - 1)))

    wait_y(second_y)
    for copy in second_x:
        copy.wait()
    run(finish(ends))
    packed = packed_stencil(
        own[...], (lam[0], lam[width_x + 1]), (widen(z_recv[0]), widen(z_recv[1])), 3, 4, 1, 6)
    own[...] = packed
    near_edge = ((lane < 2) | (lane >= width_y - 2))[:8]
    for b in range(bins):
        for x in range(0, width_x, 8):
            here = slice(b * width_x + x, b * width_x + x + 8)
            cells = jnp.broadcast_to(own[b:b + 1, :], (8, width_y))
            cells = pltpu.roll(cells, width_y - shift_of(x), 1, stride=span, stride_axis=0)
            out[here, :] = jnp.where(near_edge, cells, out[here, :])


def body(n_gx, n_gy, concentration, adjoint_next, sign_x, sign_y, courant_x, courant_y, active, kernel_a, kernel_b):
    bins, width_x, width_y = concentration.shape
    cells = bins * width_x
    depth = bins * 2 * width_x // width_y
    tables = dft_tables(bins)
    operands = (
        concentration.reshape(cells, width_y),
        adjoint_next.reshape(cells, width_y),
        sign_x, sign_y, courant_x, courant_y, active,
        kernel_a.reshape(1, bins), kernel_b.reshape(1, bins),
        *(jnp.asarray(t) for t in tables),
    )
    result = pl.pallas_call(
        functools.partial(kernel, n_gx, n_gy, width_x),
        out_shape=pltpu.VMEM((cells, width_y), F32),
        in_specs=[pl.BlockSpec(memory_space=pltpu.HBM)] * 12,
        out_specs=pl.BlockSpec(memory_space=pltpu.VMEM),
        scratch_shapes=[
            *(pltpu.VMEM(a.shape, a.dtype) for a in operands),
            pltpu.VMEM((cells, width_y), F32),
            pltpu.VMEM((cells, width_y), F32),
            pltpu.VMEM((width_x + 2, bins + 8, width_y), F32),
            pltpu.VMEM((width_x + 2, bins, width_y), F32),
            pltpu.VMEM((depth + 8, width_y), F32),
            pltpu.VMEM((2, depth + 8, width_y), F32),
            pltpu.VMEM((depth, width_y), F32),
            pltpu.VMEM((2, depth, width_y), F32),
            pltpu.VMEM((bins, width_y), F32),
            pltpu.VMEM((16 * width_x, width_y), F32),
            pltpu.VMEM((16, width_y), F32),
            pltpu.VMEM((4 * bins + 5 * PART, 2 * bins), BF16),
            pltpu.VMEM((bins, 2 * bins + 4 * PART), BF16),
            pltpu.VMEM((2 * bins + 2 * PART, 2 * bins), BF16),
            pltpu.VMEM((bins, 4 * bins + 8 * PART), BF16),
            pltpu.VMEM((2, bins, bins), F32),
            pltpu.SemaphoreType.DMA((8,)),
            pltpu.SemaphoreType.DMA((8,)),
            pltpu.SemaphoreType.DMA((12,)),
        ],
        compiler_params=pltpu.CompilerParams(
            collective_id=0, has_side_effects=True, vmem_limit_bytes=60 * 1024 * 1024
        ),
    )(*operands)
    return result.reshape(bins, width_x, width_y)


def solution(mesh):
    return jax.shard_map(
        functools.partial(body, mesh.shape["gx"], mesh.shape["gy"]),
        mesh=mesh,
        in_specs=(
            P(None, "gx", "gy"),
            P(None, "gx", "gy"),
            P("gx", "gy"),
            P("gx", "gy"),
            P("gx", "gy"),
            P("gx", "gy"),
            P("gx", "gy"),
            P(),
            P(),
        ),
        out_specs=P(None, "gx", "gy"),
        check_vma=False,
    )
```
